32 devices in a mesh: ev: 2 (over y), gx: 4 (over z), gy: 4 (over x, core).
Axes of the slice: x: 2, y: 2, z: 4, core: 2. Of those that a mesh axis runs over, the one named last changes fastest.
Arguments:
- forward_state: float32 [2, 9, 4, 64, 512], P('ev', None, None, 'gx', 'gy'), may hold values from -6 to 6
- adjoint_state: float32 [2, 9, 4, 64, 512], P('ev', None, None, 'gx', 'gy'), may hold values from -6 to 6
- first_lame_parameter: float32 [4, 64, 512], P(None, 'gx', 'gy'), may hold values from 0.5 to 2
- shear_stiffness: float32 [4, 64, 512], P(None, 'gx', 'gy'), may hold values from 0.5 to 1.5
- buoyancy: float32 [4, 64, 512], P(None, 'gx', 'gy'), may hold values from 0.5 to 1.5
- layer_mask: int32 [4, 64, 512], P(None, 'gx', 'gy'), may hold values 0 or 1
- layer_element: int32 [4, 64, 512], P(None, 'gx', 'gy'), may hold values from 0 to 511
- layer_forces: float32 [2, 3, 512], P('ev'), may hold values from -24 to 24
Outputs:
- forward_next: float32 [2, 9, 4, 64, 512], P('ev', None, None, 'gx', 'gy')
- kernels: float32 [3, 4, 64, 512], P(None, None, 'gx', 'gy')
The draws below stay inside these ranges and needn't reach their ends.
All inputs are finite; a program needn't handle non-finite values. No bound on the sum of `layer_mask` on one device may be relied on, other than what follows from the above.
Results may differ from the reference program's by a relative error of at most 0.00002.
Values sent between devices are 32-bit elements; how exact they have to be, the bound alone decides.
A program may use at most 64 MiB of HBM per device.

```python
import math
import jax
import jax.numpy as jnp
from jax import lax

Z = 4
NELEM = 512
EVENTS = 2
NX = 64
NY = 512


def draw_wavefield(key, salt):
    inner_key = jax.random.fold_in(key, salt)
    shape = (EVENTS, 9, Z, NX, NY)
    values = jnp.clip(jax.random.normal(inner_key, shape, jnp.float32), -6.0, 6.0)
    factor = jnp.where(jnp.arange(9) < 3, 0.1, 1.0).astype(jnp.float32)
    return values * factor[None, :, None, None, None]


def draw_forward_state(key, part):
    return draw_wavefield(key, 11)


def draw_adjoint_state(key, part):
    return draw_wavefield(key, 23)


def touch_ends(values, key, least, high):
    index_at = [jax.random.randint(jax.random.fold_in(key, axis), (), 0, length) for axis, length in enumerate(values.shape)]
    longest = values.shape.index(max(values.shape))
    next_to = index_at[:longest] + [(index_at[longest] + 1) % values.shape[longest]] + index_at[longest + 1:]
    return values.at[tuple(index_at)].set(least).at[tuple(next_to)].set(high)


def level_of(stream_key, dims, split, smallest, high):
    gain = 1.0
    for dim, parts in split:
        draws = jax.random.uniform(jax.random.fold_in(jax.random.fold_in(stream_key, 6), dim), (parts,), jnp.float32, smallest / len(split), high / len(split))
        gain = gain * jnp.repeat(jnp.exp(draws), dims[dim] // parts).reshape((-1,) + (1,) * (len(dims) - 1 - dim))
    return gain


def noise(key, dims, deviation, reach, shards=(), held_as=jnp.bfloat16):
    level = level_of(key, dims, shards, -0.22, 0.18) if shards else 1.0
    drawn = jax.random.normal(key, dims, jnp.float32) * deviation * level
    return jnp.minimum(jnp.maximum(drawn, -reach), reach).astype(held_as)


def setup_inputs(seed: int = 0) -> dict:
    streams_of = jax.random.split(jax.random.key(seed), 9)
    return {
        "forward_state": draw_forward_state(jax.random.fold_in(streams_of[8], 71), 0),
        "adjoint_state": draw_adjoint_state(jax.random.fold_in(streams_of[8], 71), 0),
        "first_lame_parameter": jnp.clip(jnp.exp(math.log(2.0) - 1.3862944 * jax.random.uniform(streams_of[2], (Z, NX, NY), jnp.float32) ** level_of(streams_of[2], (Z, NX, NY), ((1, 4), (2, 4)), -0.2, 0.2)), 0.5, 2.0),
        "shear_stiffness": jnp.clip(jnp.exp(math.log(1.5) - 1.0986123 * jax.random.uniform(streams_of[3], (Z, NX, NY), jnp.float32) ** level_of(streams_of[3], (Z, NX, NY), ((1, 4), (2, 4)), -0.2, 0.2)), 0.5, 1.5),
        "buoyancy": jnp.clip(jnp.exp(math.log(1.5) - 1.0986123 * jax.random.uniform(streams_of[4], (Z, NX, NY), jnp.float32) ** level_of(streams_of[4], (Z, NX, NY), ((1, 4), (2, 4)), -0.2, 0.2)), 0.5, 1.5),
        "layer_mask": touch_ends((jax.random.randint(streams_of[5], (Z, NX, NY), 0, 2) < 1).astype(jnp.int32), jax.random.fold_in(streams_of[5], 1), 0, 1),
        "layer_element": touch_ends(jax.random.randint(streams_of[6], (Z, NX, NY), 0, NELEM), jax.random.fold_in(streams_of[6], 1), 0, NELEM - 1).astype(jnp.int32),
        "layer_forces": noise(streams_of[7], (EVENTS, 3, NELEM), 4.0, 24.0, ((0, 2),), jnp.float32),
    }


inner_coeff = 9.0 / 8.0
outer_coeff = -1.0 / 24.0
advance_time_step = 0.15
axis_of = (1, 2, 0)


def stress_slot(first, second):
    if first == second:
        return first
    return {(0, 1): 3, (1, 0): 3, (0, 2): 4, (2, 0): 4, (1, 2): 5, (2, 1): 5}[(first, second)]


def window(padded, direction, offset):
    starts = [2, 2, 2]
    starts[direction] = 2 + offset
    limits = [starts[dimension] + padded.shape[dimension] - 4 for dimension in range(3)]
    return lax.slice(padded, starts, limits)


def ahead_diff(padded, direction):
    return inner_coeff * (window(padded, direction, 1) - window(padded, direction, 0)) + outer_coeff * (window(padded, direction, 2) - window(padded, direction, -1))


def behind_diff(padded, direction):
    return inner_coeff * (window(padded, direction, 0) - window(padded, direction, -1)) + outer_coeff * (window(padded, direction, 1) - window(padded, direction, -2))


def move_velocity(velocity, padded_stress, buoyancy, forcing, step_now):
    result = []
    for first in range(3):
        pieces = []
        for second in range(3):
            component = padded_stress[stress_slot(first, second)]
            if first == second:
                pieces.append(behind_diff(component, axis_of[second]))
            else:
                pieces.append(ahead_diff(component, axis_of[second]))
        updated = velocity[first] + step_now * (buoyancy * (pieces[0] + pieces[1] + pieces[2]))
        if forcing is not None:
            updated = updated + step_now * forcing[first]
        result.append(updated)
    return jnp.stack(result)


def advance_stress(stress, padded_velocity, first_lame_parameter, shear_stiffness, step_now):
    normal_rates = [ahead_diff(padded_velocity[first], axis_of[first]) for first in range(3)]
    dilatation = normal_rates[0] + normal_rates[1] + normal_rates[2]
    updated = [stress[first] + step_now * (first_lame_parameter * dilatation + 2.0 * shear_stiffness * normal_rates[first]) for first in range(3)]
    shears = []
    for first, second in ((0, 1), (0, 2), (1, 2)):
        shear_rate = behind_diff(padded_velocity[first], axis_of[second]) + behind_diff(padded_velocity[second], axis_of[first])
        updated.append(stress[3 + len(shears)] + step_now * shear_stiffness * shear_rate)
        shears.append(shear_rate)
    return jnp.stack(updated), normal_rates, dilatation, shears


def imaging_condition(forward_pieces_list, adjoint_pieces_list, forward_velocity_field, adjoint_velocity_field, adjoint_before):
    forward_strain_rates, forward_divergence, forward_shear_terms = forward_pieces_list
    adjoint_strain_rates, adjoint_divergence, adjoint_shear_terms = adjoint_pieces_list
    lambda_sensitivity = forward_divergence * adjoint_divergence
    modulus_term = 2.0 * (forward_strain_rates[0] * adjoint_strain_rates[0] + forward_strain_rates[1] * adjoint_strain_rates[1] + forward_strain_rates[2] * adjoint_strain_rates[2])
    modulus_term = modulus_term + forward_shear_terms[0] * adjoint_shear_terms[0] + forward_shear_terms[1] * adjoint_shear_terms[1] + forward_shear_terms[2] * adjoint_shear_terms[2]
    density_term = forward_velocity_field[0] * (adjoint_velocity_field[0] - adjoint_before[0]) + forward_velocity_field[1] * (adjoint_velocity_field[1] - adjoint_before[1]) + forward_velocity_field[2] * (adjoint_velocity_field[2] - adjoint_before[2])
    return jnp.stack([lambda_sensitivity, modulus_term, density_term / advance_time_step])


def pad_every_field(values):
    return jnp.pad(values, ((0, 0), (2, 2), (2, 2), (2, 2)))


def reference(forward_state, adjoint_state, first_lame_parameter, shear_stiffness, buoyancy, layer_mask, layer_element, layer_forces):
    mask_float = layer_mask.astype(jnp.float32)
    outputs = []
    kernels = jnp.zeros((3,) + first_lame_parameter.shape, jnp.float32)
    for member in range(EVENTS):
        forward_wavefield = forward_state[member]
        adjoint_wavefield = adjoint_state[member]
        forcing = jnp.stack([mask_float * jnp.take(layer_forces[member, first], layer_element) for first in range(3)])
        forward_velocity_field = move_velocity(forward_wavefield[:3], pad_every_field(forward_wavefield[3:]), buoyancy, forcing, advance_time_step)
        adjoint_velocity_field = move_velocity(adjoint_wavefield[:3], pad_every_field(adjoint_wavefield[3:]), buoyancy, None, -advance_time_step)
        forward_stress_field, forward_strain_rates, forward_divergence, forward_shear_terms = advance_stress(forward_wavefield[3:], pad_every_field(forward_velocity_field), first_lame_parameter, shear_stiffness, advance_time_step)
        adjoint_stress_field, adjoint_strain_rates, adjoint_divergence, adjoint_shear_terms = advance_stress(adjoint_wavefield[3:], pad_every_field(adjoint_velocity_field), first_lame_parameter, shear_stiffness, -advance_time_step)
        sensitivity_terms = imaging_condition((forward_strain_rates, forward_divergence, forward_shear_terms), (adjoint_strain_rates, adjoint_divergence, adjoint_shear_terms), forward_velocity_field, adjoint_velocity_field, adjoint_wavefield[:3])
        kernels = kernels + sensitivity_terms
        outputs.append(jnp.concatenate([forward_velocity_field, forward_stress_field], 0))
    return jnp.stack(outputs), kernels
```

```python
import functools

import jax
import jax.numpy as jnp
from jax import lax
from jax.experimental import pallas as pl
from jax.experimental.pallas import tpu as pltpu
from jax.sharding import PartitionSpec as P

MESH = pl.DeviceIdType.MESH
INNER = 9.0 / 8.0
OUTER = -1.0 / 24.0
STEP = 0.15
PAD = 8


def depth_ahead(f):
    zero = jnp.zeros_like(f[:, :1])
    p1 = jnp.concatenate([f[:, 1:], zero], 1)
    p2 = jnp.concatenate([f[:, 2:], zero, zero], 1)
    m1 = jnp.concatenate([zero, f[:, :-1]], 1)
    return INNER * (p1 - f) + OUTER * (p2 - m1)


def depth_behind(f):
    zero = jnp.zeros_like(f[:, :1])
    p1 = jnp.concatenate([f[:, 1:], zero], 1)
    m1 = jnp.concatenate([zero, f[:, :-1]], 1)
    m2 = jnp.concatenate([zero, zero, f[:, :-2]], 1)
    return INNER * (f - m1) + OUTER * (p1 - m2)


def turn(f, shift):
    return pltpu.roll(f, shift % f.shape[-1], f.ndim - 1)


def lane_ahead(f):
    return INNER * (turn(f, -1) - f) + OUTER * (turn(f, -2) - turn(f, 1))


def lane_behind(f):
    return INNER * (f - turn(f, 1)) + OUTER * (turn(f, -1) - turn(f, 2))


def row_ahead(ref, c, rows):
    def at(k):
        return ref[:, c, :, pl.ds(PAD + k, rows), :]

    return INNER * (at(1) - at(0)) + OUTER * (at(2) - at(-1))


def row_behind(ref, c, rows):
    def at(k):
        return ref[:, c, :, pl.ds(PAD + k, rows), :]

    return INNER * (at(0) - at(-1)) + OUTER * (at(1) - at(-2))


def pack_lanes(fields, lanes):
    slot_of = lanes // 4
    packed = jnp.zeros(lanes.shape, jnp.float32)
    k = 0
    for f in fields:
        for s in range(f.shape[0]):
            for z in range(f.shape[1]):
                packed = jnp.where(slot_of == k, turn(f[s, z], 4 * k + 2), packed)
                k += 1
    return packed


def lane_fix(own, left, right, lanes, per, ahead):
    place = lanes % 4
    kind = lanes // (4 * per)
    is_ahead = functools.reduce(
        jnp.logical_or, [kind == c for c, flag in enumerate(ahead) if flag]
    )

    def weight(ahead_at, behind_at):
        def table(entries):
            out = jnp.zeros(lanes.shape, jnp.float32)
            for j, value in entries:
                out = jnp.where(place == j, value, out)
            return out

        return jnp.where(is_ahead, table(ahead_at), table(behind_at))

    m = jnp.where(place < 2, left, right) - own
    return (
        weight([(0, OUTER), (1, OUTER)], []) * turn(m, -2)
        + weight([(1, INNER)], [(1, OUTER)]) * turn(m, -1)
        + weight([(2, -OUTER)], [(2, -INNER)]) * turn(m, 1)
        + weight([], [(2, -OUTER), (3, -OUTER)]) * turn(m, 2)
    )


def unpack_lanes(fix, first, count, depth, edge):
    parts = []
    for s in range(2):
        parts.append(
            jnp.stack(
                [
                    jnp.where(edge, turn(fix, -(4 * (first + s * depth + z) + 2)), 0.0)
                    for z in range(depth)
                ]
            )
        )
    return jnp.stack(parts)


def kernel(
    sizes,
    fwd,
    adj,
    lame_in,
    shear_in,
    buoy_in,
    mask_in,
    elem_in,
    table_in,
    out,
    grad,
    ext,
    rest,
    lame,
    shear,
    buoy,
    mask,
    elem,
    table,
    vext,
    sums,
    pack,
    from_left,
    from_right,
    mine,
    theirs,
    stress,
    total,
    load_sem,
    store_sem,
    row_send,
    row_recv,
    lane_send,
    lane_recv,
    ev_send,
    ev_recv,
):
    n_ev, n_gx, n_gy = sizes
    ev, gx, gy = lax.axis_index("ev"), lax.axis_index("gx"), lax.axis_index("gy")
    _, _, depth, rows, cols = rest.shape
    per = 2 * depth

    barrier = pltpu.get_barrier_semaphore()
    has = {
        "up": gx > 0,
        "down": gx < n_gx - 1,
        "left": gy > 0,
        "right": gy < n_gy - 1,
    }
    where = {
        "up": {"gx": gx - 1},
        "down": {"gx": gx + 1},
        "left": {"gy": gy - 1},
        "right": {"gy": gy + 1},
    }
    mates = [{"ev": lax.rem(ev + d, n_ev)} for d in range(1, n_ev)]

    loads = {}

    def load(name, src, dst):
        copy = pltpu.make_async_copy(src, dst, load_sem.at[len(loads)])
        loads[name] = copy
        copy.start()

    for s, state in enumerate((fwd, adj)):
        load(("n0", s), state.at[0, pl.ds(3, 1)], ext.at[s, pl.ds(0, 1), :, pl.ds(PAD, rows), :])
        load(("n1", s), state.at[0, pl.ds(6, 2)], ext.at[s, pl.ds(1, 2), :, pl.ds(PAD, rows), :])
        load(("s0", s), state.at[0, pl.ds(4, 2)], rest.at[s, pl.ds(3, 2)])
        load(("s1", s), state.at[0, pl.ds(8, 1)], rest.at[s, pl.ds(5, 1)])
    for s, state in enumerate((fwd, adj)):
        load(("v", s), state.at[0, pl.ds(0, 3)], rest.at[s, pl.ds(0, 3)])
    load("table", table_in.at[0], table)
    load("elem", elem_in, elem)
    load("mask", mask_in, mask)
    load("buoy", buoy_in, buoy)
    load("lame", lame_in, lame)
    load("shear", shear_in, shear)

    for side in has:

        @pl.when(has[side])
        def _(side=side):
            pl.semaphore_signal(barrier, inc=1, device_id=where[side], device_id_type=MESH)

    for mate in mates:
        pl.semaphore_signal(barrier, inc=1, device_id=mate, device_id_type=MESH)

    @pl.when(gx == 0)
    def _():
        for ref in (ext, vext):
            ref[:, :, :, pl.ds(0, PAD), :] = jnp.zeros(ref.shape[:3] + (PAD, cols), jnp.float32)

    @pl.when(gx == n_gx - 1)
    def _():
        for ref in (ext, vext):
            ref[:, :, :, pl.ds(PAD + rows, PAD), :] = jnp.zeros(
                ref.shape[:3] + (PAD, cols), jnp.float32
            )

    @pl.when(gy == 0)
    def _():
        from_left[...] = jnp.zeros(from_left.shape, jnp.float32)

    @pl.when(gy == n_gy - 1)
    def _():
        from_right[...] = jnp.zeros(from_right.shape, jnp.float32)

    for s in range(2):
        for name in ("n0", "n1", "s0", "s1"):
            loads[name, s].wait()

    lanes = lax.broadcasted_iota(jnp.int32, (rows, cols), 1)
    edge = jnp.logical_or(lanes < 2, lanes >= cols - 2)

    def inside(ref, c):
        return ref[:, c, :, pl.ds(PAD, rows), :]

    def row_copy(ref, phase, side):
        start, goal = (PAD + rows - 2, PAD - 2) if side == "down" else (PAD, PAD + rows)
        i = 2 * phase + (side == "down")
        return pltpu.make_async_remote_copy(
            src_ref=ref.at[:, :, :, pl.ds(start, 2), :],
            dst_ref=ref.at[:, :, :, pl.ds(goal, 2), :],
            send_sem=row_send.at[i],
            recv_sem=row_recv.at[i],
            device_id=where[side],
            device_id_type=MESH,
        )

    def lane_copy(phase, side):
        i = 2 * phase + (side == "right")
        return pltpu.make_async_remote_copy(
            src_ref=pack.at[phase],
            dst_ref=(from_left if side == "right" else from_right).at[phase],
            send_sem=lane_send.at[i],
            recv_sem=lane_recv.at[i],
            device_id=where[side],
            device_id_type=MESH,
        )

    opposite = {"up": "down", "down": "up", "left": "right", "right": "left"}

    def copy_of(phase, side):
        if side in ("up", "down"):
            return row_copy((ext, vext)[phase], phase, side)
        return lane_copy(phase, side)

    def send(phase, sides):
        for side in sides:

            @pl.when(has[side])
            def _(side=side):
                copy_of(phase, side).start()

    def receive(phase, sides):
        for side in sides:

            @pl.when(has[side])
            def _(side=side):
                copy_of(phase, opposite[side]).wait_recv()

    def sent(phase):
        for side in has:

            @pl.when(has[side])
            def _(side=side):
                copy_of(phase, side).wait_send()

    sxy, syy, syz = inside(ext, 1), rest[:, 3], rest[:, 5]
    pack[0] = pack_lanes((sxy, syy, syz), lanes)

    peers = len(mates) + sum(flag.astype(jnp.int32) for flag in has.values())
    pl.semaphore_wait(barrier, peers)

    send(0, ("up", "down", "left", "right"))

    sums[0] = lane_ahead(sxy) + depth_ahead(inside(ext, 2))
    sums[1] = lane_behind(syy) + depth_ahead(syz)
    sums[2] = lane_ahead(syz) + depth_behind(rest[:, 4])

    for name in (("v", 0), ("v", 1), "table", "elem", "mask", "buoy"):
        loads[name].wait()
    entries = table.shape[1]
    chunks = [(a, min(a + cols, entries)) for a in range(0, entries, cols)]
    for z in range(depth):
        index = elem[z]
        gate = STEP * mask[z].astype(jnp.float32)
        low, high = index % cols, index // cols
        for i in range(3):
            value = jnp.zeros((rows, cols), jnp.float32)
            for j, (a, b) in enumerate(chunks):
                line = jnp.broadcast_to(table[pl.ds(i, 1), pl.ds(a, b - a)], (rows, cols))
                value = jnp.where(high == j, jnp.take_along_axis(line, low, axis=1), value)
            rest[0, i, z] = rest[0, i, z] + gate * value

    receive(0, ("up", "down", "left", "right"))
    fix = lane_fix(pack[0], from_left[0], from_right[0], lanes, per, (True, False, True))
    force = buoy[...] * STEP
    force = jnp.stack([force, -force])
    row_diff = (row_behind, row_ahead, row_ahead)
    for i in range(3):
        divergence = (
            sums[i]
            + row_diff[i](ext, i, rows)
            + unpack_lanes(fix, i * per, per, depth, edge)
        )
        vext[:, i, :, pl.ds(PAD, rows), :] = rest[:, i] + force * divergence

    velocity = [inside(vext, i) for i in range(3)]
    pack[1] = pack_lanes(velocity, lanes)
    send(1, ("up", "down", "left", "right"))

    def mate_copy(d, part):
        return pltpu.make_async_remote_copy(
            src_ref=mine.at[part],
            dst_ref=theirs.at[d, part],
            send_sem=ev_send.at[d, part],
            recv_sem=ev_recv.at[d, part],
            device_id=mates[d],
            device_id_type=MESH,
        )

    def store(i, src, dst):
        copy = pltpu.make_async_copy(src, dst, store_sem.at[i])
        copy.start()
        return copy

    stores = [store(0, vext.at[0, :, :, pl.ds(PAD, rows), :], out.at[0, pl.ds(0, 3)])]

    vx, vy, vz = velocity
    mine[2] = (
        vx[0] * (vx[1] - rest[1, 0]) + vy[0] * (vy[1] - rest[1, 1]) + vz[0] * (vz[1] - rest[1, 2])
    ) / STEP
    for d in range(len(mates)):
        mate_copy(d, 2).start()

    sums[0] = lane_behind(vx)
    sums[1] = lane_ahead(vy)
    sums[2] = lane_behind(vz) + depth_behind(vy)
    rate_z = depth_ahead(vz)
    shear_xz = depth_behind(vx)
    loads["lame"].wait()
    loads["shear"].wait()

    receive(1, ("up", "down", "left", "right"))
    fix = lane_fix(pack[1], from_left[1], from_right[1], lanes, per, (False, True, False))
    rate_x = row_ahead(vext, 0, rows)
    rate_y = sums[1] + unpack_lanes(fix, per, per, depth, edge)
    dilatation = rate_x + rate_y + rate_z
    mine[0] = dilatation[0] * dilatation[1]
    for d in range(len(mates)):
        mate_copy(d, 0).start()
    shear_xy = sums[0] + unpack_lanes(fix, 0, per, depth, edge) + row_behind(vext, 1, rows)
    shear_xz = shear_xz + row_behind(vext, 2, rows)
    shear_yz = sums[2] + unpack_lanes(fix, 2 * per, per, depth, edge)
    mine[1] = (
        2.0 * (rate_x[0] * rate_x[1] + rate_y[0] * rate_y[1] + rate_z[0] * rate_z[1])
        + shear_xy[0] * shear_xy[1]
        + shear_xz[0] * shear_xz[1]
        + shear_yz[0] * shear_yz[1]
    )
    for d in range(len(mates)):
        mate_copy(d, 1).start()

    mu = STEP * shear[...]
    bulk = STEP * lame[...] * dilatation[0]
    stress[0] = ext[0, 0, :, pl.ds(PAD, rows), :] + (bulk + 2.0 * mu * rate_x[0])
    stress[1] = rest[0, 3] + (bulk + 2.0 * mu * rate_y[0])
    stress[2] = rest[0, 4] + (bulk + 2.0 * mu * rate_z[0])
    stress[3] = ext[0, 1, :, pl.ds(PAD, rows), :] + mu * shear_xy[0]
    stress[4] = ext[0, 2, :, pl.ds(PAD, rows), :] + mu * shear_xz[0]
    stress[5] = rest[0, 5] + mu * shear_yz[0]
    stores.append(store(1, stress, out.at[0, pl.ds(3, 6)]))

    for n, part in enumerate((2, 0, 1)):
        value = mine[part]
        for d in range(len(mates)):
            mate_copy(d, part).wait_recv()
            value = value + theirs[d, part]
        total[part] = value
        stores.append(store(2 + n, total.at[part], grad.at[part]))

    sent(0)
    sent(1)
    for d in range(len(mates)):
        for part in range(3):
            mate_copy(d, part).wait_send()
    for copy in stores:
        copy.wait()


def solution(mesh):
    sizes = (mesh.shape["ev"], mesh.shape["gx"], mesh.shape["gy"])

    def shards(fwd, adj, lame, shear, buoy, mask, elem, table):
        _, comps, depth, rows, cols = fwd.shape
        block = (depth, rows, cols)
        padded = (2, 3, depth, rows + 2 * PAD, cols)
        mates = max(sizes[0] - 1, 1)
        f32 = jnp.float32
        dma = pltpu.SemaphoreType.DMA
        anywhere = pl.BlockSpec(memory_space=pl.ANY)
        return pl.pallas_call(
            functools.partial(kernel, sizes),
            out_shape=(
                jax.ShapeDtypeStruct(fwd.shape, f32),
                jax.ShapeDtypeStruct((3,) + block, f32),
            ),
            in_specs=[anywhere] * 8,
            out_specs=(anywhere, anywhere),
            scratch_shapes=[
                pltpu.VMEM(padded, f32),
                pltpu.VMEM((2, 6) + block, f32),
                pltpu.VMEM(block, f32),
                pltpu.VMEM(block, f32),
                pltpu.VMEM(block, f32),
                pltpu.VMEM(block, jnp.int32),
                pltpu.VMEM(block, jnp.int32),
                pltpu.VMEM(table.shape[1:], f32),
                pltpu.VMEM(padded, f32),
                pltpu.VMEM((3, 2) + block, f32),
                pltpu.VMEM((2, rows, cols), f32),
                pltpu.VMEM((2, rows, cols), f32),
                pltpu.VMEM((2, rows, cols), f32),
                pltpu.VMEM((3,) + block, f32),
                pltpu.VMEM((mates, 3) + block, f32),
                pltpu.VMEM((6,) + block, f32),
                pltpu.VMEM((3,) + block, f32),
                dma((16,)),
                dma((5,)),
                dma((4,)),
                dma((4,)),
                dma((4,)),
                dma((4,)),
                dma((mates, 3)),
                dma((mates, 3)),
            ],
            compiler_params=pltpu.CompilerParams(
                collective_id=0, has_side_effects=True, vmem_limit_bytes=24 * 1024 * 1024
            ),
        )(fwd, adj, lame, shear, buoy, mask, elem, table)

    grid = P(None, "gx", "gy")
    state = P("ev", None, None, "gx", "gy")
    return jax.shard_map(
        shards,
        mesh=mesh,
        in_specs=(state, state, grid, grid, grid, grid, grid, P("ev", None, None)),
        out_specs=(state, P(None, None, "gx", "gy")),
        check_vma=False,
    )
```

```python
import functools

import jax
import jax.numpy as jnp
from jax import lax
from jax.experimental import pallas as pl
from jax.experimental.pallas import tpu as pltpu
from jax.sharding import PartitionSpec as P

MESH = pl.DeviceIdType.MESH
INNER = 9.0 / 8.0
OUTER = -1.0 / 24.0
STEP = 0.15
PAD = 8


def depth_ahead(f):
    zero = jnp.zeros_like(f[:, :1])
    p1 = jnp.concatenate([f[:, 1:], zero], 1)
    p2 = jnp.concatenate([f[:, 2:], zero, zero], 1)
    m1 = jnp.concatenate([zero, f[:, :-1]], 1)
    return INNER * (p1 - f) + OUTER * (p2 - m1)


def depth_behind(f):
    zero = jnp.zeros_like(f[:, :1])
    p1 = jnp.concatenate([f[:, 1:], zero], 1)
    m1 = jnp.concatenate([zero, f[:, :-1]], 1)
    m2 = jnp.concatenate([zero, zero, f[:, :-2]], 1)
    return INNER * (f - m1) + OUTER * (p1 - m2)


def turn(f, shift):
    return pltpu.roll(f, shift % f.shape[-1], f.ndim - 1)


def lane_ahead(f):
    return INNER * (turn(f, -1) - f) + OUTER * (turn(f, -2) - turn(f, 1))


def lane_behind(f):
    return INNER * (f - turn(f, 1)) + OUTER * (turn(f, -1) - turn(f, 2))


def row_ahead(ref, c, rows):
    def at(k):
        return ref[:, c, :, pl.ds(PAD + k, rows), :]

    return INNER * (at(1) - at(0)) + OUTER * (at(2) - at(-1))


def row_behind(ref, c, rows):
    def at(k):
        return ref[:, c, :, pl.ds(PAD + k, rows), :]

    return INNER * (at(0) - at(-1)) + OUTER * (at(1) - at(-2))


def pack_lanes(fields, lanes):
    slot_of = lanes // 4
    packed = jnp.zeros(lanes.shape, jnp.float32)
    k = 0
    for f in fields:
        for s in range(f.shape[0]):
            for z in range(f.shape[1]):
                packed = jnp.where(slot_of == k, turn(f[s, z], 4 * k + 2), packed)
                k += 1
    return packed


def lane_fix(own, left, right, lanes, per, ahead):
    place = lanes % 4
    kind = lanes // (4 * per)
    is_ahead = functools.reduce(
        jnp.logical_or, [kind == c for c, flag in enumerate(ahead) if flag]
    )

    def weight(ahead_at, behind_at):
        def table(entries):
            out = jnp.zeros(lanes.shape, jnp.float32)
            for j, value in entries:
                out = jnp.where(place == j, value, out)
            return out

        return jnp.where(is_ahead, table(ahead_at), table(behind_at))

    m = jnp.where(place < 2, left, right) - own
    return (
        weight([(0, OUTER), (1, OUTER)], []) * turn(m, -2)
        + weight([(1, INNER)], [(1, OUTER)]) * turn(m, -1)
        + weight([(2, -OUTER)], [(2, -INNER)]) * turn(m, 1)
        + weight([], [(2, -OUTER), (3, -OUTER)]) * turn(m, 2)
    )


def unpack_lanes(fix, first, count, depth, edge):
    parts = []
    for s in range(2):
        parts.append(
            jnp.stack(
                [
                    jnp.where(edge, turn(fix, -(4 * (first + s * depth + z) + 2)), 0.0)
                    for z in range(depth)
                ]
            )
        )
    return jnp.stack(parts)


def kernel(
    sizes,
    fwd,
    adj,
    lame_in,
    shear_in,
    buoy_in,
    mask_in,
    elem_in,
    table_in,
    out,
    grad,
    ext,
    rest,
    lame,
    shear,
    buoy,
    mask,
    elem,
    table,
    vext,
    sums,
    pack,
    from_left,
    from_right,
    mine,
    theirs,
    stress,
    total,
    load_sem,
    store_sem,
    row_send,
    row_recv,
    lane_send,
    lane_recv,
    ev_send,
    ev_recv,
):
    n_ev, n_gx, n_gy = sizes
    ev, gx, gy = lax.axis_index("ev"), lax.axis_index("gx"), lax.axis_index("gy")
    _, _, depth, rows, cols = rest.shape
    per = 2 * depth

    barrier = pltpu.get_barrier_semaphore()
    has = {
        "up": gx > 0,
        "down": gx < n_gx - 1,
        "left": gy > 0,
        "right": gy < n_gy - 1,
    }
    where = {
        "up": {"gx": gx - 1},
        "down": {"gx": gx + 1},
        "left": {"gy": gy - 1},
        "right": {"gy": gy + 1},
    }
    mates = [{"ev": lax.rem(ev + d, n_ev)} for d in range(1, n_ev)]

    loads = {}

    def load(name, src, dst):
        copy = pltpu.make_async_copy(src, dst, load_sem.at[len(loads)])
        loads[name] = copy
        copy.start()

    for s, state in enumerate((fwd, adj)):
        load(("n0", s), state.at[0, pl.ds(3, 1)], ext.at[s, pl.ds(0, 1), :, pl.ds(PAD, rows), :])
        load(("n1", s), state.at[0, pl.ds(6, 2)], ext.at[s, pl.ds(1, 2), :, pl.ds(PAD, rows), :])
        load(("s0", s), state.at[0, pl.ds(4, 2)], rest.at[s, pl.ds(3, 2)])
        load(("s1", s), state.at[0, pl.ds(8, 1)], rest.at[s, pl.ds(5, 1)])
    for s, state in enumerate((fwd, adj)):
        load(("v", s), state.at[0, pl.ds(0, 3)], rest.at[s, pl.ds(0, 3)])
    load("table", table_in, table)
    load("elem", elem_in, elem)
    load("mask", mask_in, mask)
    load("buoy", buoy_in, buoy)
    load("lame", lame_in, lame)
    load("shear", shear_in, shear)

    for side in has:

        @pl.when(has[side])
        def _(side=side):
            pl.semaphore_signal(barrier, inc=1, device_id=where[side], device_id_type=MESH)

    for mate in mates:
        pl.semaphore_signal(barrier, inc=1, device_id=mate, device_id_type=MESH)

    @pl.when(gx == 0)
    def _():
        for ref in (ext, vext):
            ref[:, :, :, pl.ds(0, PAD), :] = jnp.zeros(ref.shape[:3] + (PAD, cols), jnp.float32)

    @pl.when(gx == n_gx - 1)
    def _():
        for ref in (ext, vext):
            ref[:, :, :, pl.ds(PAD + rows, PAD), :] = jnp.zeros(
                ref.shape[:3] + (PAD, cols), jnp.float32
            )

    @pl.when(gy == 0)
    def _():
        from_left[...] = jnp.zeros(from_left.shape, jnp.float32)

    @pl.when(gy == n_gy - 1)
    def _():
        from_right[...] = jnp.zeros(from_right.shape, jnp.float32)

    for s in range(2):
        for name in ("n0", "n1", "s0", "s1"):
            loads[name, s].wait()

    lanes = lax.broadcasted_iota(jnp.int32, (rows, cols), 1)
    edge = jnp.logical_or(lanes < 2, lanes >= cols - 2)

    def inside(ref, c):
        return ref[:, c, :, pl.ds(PAD, rows), :]

    def row_copy(ref, phase, side):
        start, goal = (PAD + rows - 2, PAD - 2) if side == "down" else (PAD, PAD + rows)
        i = 2 * phase + (side == "down")
        return pltpu.make_async_remote_copy(
            src_ref=ref.at[:, :, :, pl.ds(start, 2), :],
            dst_ref=ref.at[:, :, :, pl.ds(goal, 2), :],
            send_sem=row_send.at[i],
            recv_sem=row_recv.at[i],
            device_id=where[side],
            device_id_type=MESH,
        )

    def lane_copy(phase, side):
        i = 2 * phase + (side == "right")
        return pltpu.make_async_remote_copy(
            src_ref=pack.at[phase],
            dst_ref=(from_left if side == "right" else from_right).at[phase],
            send_sem=lane_send.at[i],
            recv_sem=lane_recv.at[i],
            device_id=where[side],
            device_id_type=MESH,
        )

    opposite = {"up": "down", "down": "up", "left": "right", "right": "left"}

    def copy_of(phase, side):
        if side in ("up", "down"):
            return row_copy((ext, vext)[phase], phase, side)
        return lane_copy(phase, side)

    def send(phase, sides):
        for side in sides:

            @pl.when(has[side])
            def _(side=side):
                copy_of(phase, side).start()

    def receive(phase, sides):
        for side in sides:

            @pl.when(has[side])
            def _(side=side):
                copy_of(phase, opposite[side]).wait_recv()

    def sent(phase):
        for side in has:

            @pl.when(has[side])
            def _(side=side):
                copy_of(phase, side).wait_send()

    sxy, syy, syz = inside(ext, 1), rest[:, 3], rest[:, 5]
    pack[0] = pack_lanes((sxy, syy, syz), lanes)

    peers = len(mates) + sum(flag.astype(jnp.int32) for flag in has.values())
    pl.semaphore_wait(barrier, peers)

    send(0, ("up", "down", "left", "right"))

    sums[0] = lane_ahead(sxy) + depth_ahead(inside(ext, 2))
    sums[1] = lane_behind(syy) + depth_ahead(syz)
    sums[2] = lane_ahead(syz) + depth_behind(rest[:, 4])

    for name in (("v", 0), ("v", 1), "table", "elem", "mask", "buoy"):
        loads[name].wait()
    entries = table.shape[2]
    chunks = [(a, min(a + cols, entries)) for a in range(0, entries, cols)]
    for z in range(depth):
        index = elem[z]
        gate = STEP * mask[z].astype(jnp.float32)
        low, high = index % cols, index // cols
        for i in range(3):
            value = jnp.zeros((rows, cols), jnp.float32)
            for j, (a, b) in enumerate(chunks):
                line = jnp.broadcast_to(table[i, :, pl.ds(a, b - a)], (rows, cols))
                value = jnp.where(high == j, jnp.take_along_axis(line, low, axis=1), value)
            rest[0, i, z] = rest[0, i, z] + gate * value

    receive(0, ("up", "down", "left", "right"))
    fix = lane_fix(pack[0], from_left[0], from_right[0], lanes, per, (True, False, True))
    force = buoy[...] * STEP
    force = jnp.stack([force, -force])
    row_diff = (row_behind, row_ahead, row_ahead)
    for i in range(3):
        divergence = (
            sums[i]
            + row_diff[i](ext, i, rows)
            + unpack_lanes(fix, i * per, per, depth, edge)
        )
        vext[:, i, :, pl.ds(PAD, rows), :] = rest[:, i] + force * divergence

    velocity = [inside(vext, i) for i in range(3)]
    pack[1] = pack_lanes(velocity, lanes)
    send(1, ("up", "down", "left", "right"))

    def mate_copy(d, part):
        return pltpu.make_async_remote_copy(
            src_ref=mine.at[part],
            dst_ref=theirs.at[d, part],
            send_sem=ev_send.at[d, part],
            recv_sem=ev_recv.at[d, part],
            device_id=mates[d],
            device_id_type=MESH,
        )

    def store(i, src, dst):
        copy = pltpu.make_async_copy(src, dst, store_sem.at[i])
        copy.start()
        return copy

    stores = [store(0, vext.at[0, :, :, pl.ds(PAD, rows), :], out.at[0, pl.ds(0, 3)])]

    vx, vy, vz = velocity
    mine[2] = (
        vx[0] * (vx[1] - rest[1, 0]) + vy[0] * (vy[1] - rest[1, 1]) + vz[0] * (vz[1] - rest[1, 2])
    ) / STEP
    for d in range(len(mates)):
        mate_copy(d, 2).start()

    sums[0] = lane_behind(vx)
    sums[1] = lane_ahead(vy)
    sums[2] = lane_behind(vz) + depth_behind(vy)
    rate_z = depth_ahead(vz)
    shear_xz = depth_behind(vx)
    loads["lame"].wait()
    loads["shear"].wait()

    receive(1, ("up", "down", "left", "right"))
    fix = lane_fix(pack[1], from_left[1], from_right[1], lanes, per, (False, True, False))
    rate_x = row_ahead(vext, 0, rows)
    rate_y = sums[1] + unpack_lanes(fix, per, per, depth, edge)
    dilatation = rate_x + rate_y + rate_z
    mine[0] = dilatation[0] * dilatation[1]
    for d in range(len(mates)):
        mate_copy(d, 0).start()
    shear_xy = sums[0] + unpack_lanes(fix, 0, per, depth, edge) + row_behind(vext, 1, rows)
    shear_xz = shear_xz + row_behind(vext, 2, rows)
    shear_yz = sums[2] + unpack_lanes(fix, 2 * per, per, depth, edge)
    mine[1] = (
        2.0 * (rate_x[0] * rate_x[1] + rate_y[0] * rate_y[1] + rate_z[0] * rate_z[1])
        + shear_xy[0] * shear_xy[1]
        + shear_xz[0] * shear_xz[1]
        + shear_yz[0] * shear_yz[1]
    )
    for d in range(len(mates)):
        mate_copy(d, 1).start()

    mu = STEP * shear[...]
    bulk = STEP * lame[...] * dilatation[0]
    stress[0] = ext[0, 0, :, pl.ds(PAD, rows), :] + (bulk + 2.0 * mu * rate_x[0])
    stress[1] = rest[0, 3] + (bulk + 2.0 * mu * rate_y[0])
    stress[2] = rest[0, 4] + (bulk + 2.0 * mu * rate_z[0])
    stress[3] = ext[0, 1, :, pl.ds(PAD, rows), :] + mu * shear_xy[0]
    stress[4] = ext[0, 2, :, pl.ds(PAD, rows), :] + mu * shear_xz[0]
    stress[5] = rest[0, 5] + mu * shear_yz[0]
    stores.append(store(1, stress, out.at[0, pl.ds(3, 6)]))

    for n, part in enumerate((2, 0, 1)):
        value = mine[part]
        for d in range(len(mates)):
            mate_copy(d, part).wait_recv()
            value = value + theirs[d, part]
        total[part] = value
        stores.append(store(2 + n, total.at[part], grad.at[part]))

    sent(0)
    sent(1)
    for d in range(len(mates)):
        for part in range(3):
            mate_copy(d, part).wait_send()
    for copy in stores:
        copy.wait()


def solution(mesh):
    sizes = (mesh.shape["ev"], mesh.shape["gx"], mesh.shape["gy"])

    def shards(fwd, adj, lame, shear, buoy, mask, elem, table):
        _, _, depth, rows, cols = fwd.shape
        table = jnp.swapaxes(table, 0, 1)
        block = (depth, rows, cols)
        padded = (2, 3, depth, rows + 2 * PAD, cols)
        mates = max(sizes[0] - 1, 1)
        f32 = jnp.float32
        dma = pltpu.SemaphoreType.DMA
        anywhere = pl.BlockSpec(memory_space=pl.ANY)
        return pl.pallas_call(
            functools.partial(kernel, sizes),
            out_shape=(
                pltpu.VMEM(fwd.shape, f32),
                pltpu.VMEM((3,) + block, f32),
            ),
            in_specs=[anywhere] * 8,
            out_specs=(anywhere, anywhere),
            scratch_shapes=[
                pltpu.VMEM(padded, f32),
                pltpu.VMEM((2, 6) + block, f32),
                pltpu.VMEM(block, f32),
                pltpu.VMEM(block, f32),
                pltpu.VMEM(block, f32),
                pltpu.VMEM(block, jnp.int32),
                pltpu.VMEM(block, jnp.int32),
                pltpu.VMEM(table.shape, f32),
                pltpu.VMEM(padded, f32),
                pltpu.VMEM((3, 2) + block, f32),
                pltpu.VMEM((2, rows, cols), f32),
                pltpu.VMEM((2, rows, cols), f32),
                pltpu.VMEM((2, rows, cols), f32),
                pltpu.VMEM((3,) + block, f32),
                pltpu.VMEM((mates, 3) + block, f32),
                pltpu.VMEM((6,) + block, f32),
                pltpu.VMEM((3,) + block, f32),
                dma((16,)),
                dma((5,)),
                dma((4,)),
                dma((4,)),
                dma((4,)),
                dma((4,)),
                dma((mates, 3)),
                dma((mates, 3)),
            ],
            compiler_params=pltpu.CompilerParams(
                collective_id=0, has_side_effects=True, vmem_limit_bytes=56 * 1024 * 1024
            ),
        )(fwd, adj, lame, shear, buoy, mask, elem, table)

    grid = P(None, "gx", "gy")
    state = P("ev", None, None, "gx", "gy")
    return jax.shard_map(
        shards,
        mesh=mesh,
        in_specs=(state, state, grid, grid, grid, grid, grid, P("ev", None, None)),
        out_specs=(state, P(None, None, "gx", "gy")),
        check_vma=False,
    )
```

```python
import functools

import jax
import jax.numpy as jnp
from jax import lax
from jax.experimental import pallas as pl
from jax.experimental.pallas import tpu as pltpu
from jax.sharding import PartitionSpec as P

MESH = pl.DeviceIdType.MESH
INNER = 9.0 / 8.0
OUTER = -1.0 / 24.0
STEP = 0.15
PAD = 8


def depth_ahead(f):
    zero = jnp.zeros_like(f[:, :1])
    p1 = jnp.concatenate([f[:, 1:], zero], 1)
    p2 = jnp.concatenate([f[:, 2:], zero, zero], 1)
    m1 = jnp.concatenate([zero, f[:, :-1]], 1)
    return INNER * (p1 - f) + OUTER * (p2 - m1)


def depth_behind(f):
    zero = jnp.zeros_like(f[:, :1])
    p1 = jnp.concatenate([f[:, 1:], zero], 1)
    m1 = jnp.concatenate([zero, f[:, :-1]], 1)
    m2 = jnp.concatenate([zero, zero, f[:, :-2]], 1)
    return INNER * (f - m1) + OUTER * (p1 - m2)


def turn(f, shift):
    return pltpu.roll(f, shift % f.shape[-1], f.ndim - 1)


def lane_ahead(f):
    return INNER * (turn(f, -1) - f) + OUTER * (turn(f, -2) - turn(f, 1))


def lane_behind(f):
    return INNER * (f - turn(f, 1)) + OUTER * (turn(f, -1) - turn(f, 2))


def row_ahead(ref, c, rows):
    def at(k):
        return ref[:, c, :, pl.ds(PAD + k, rows), :]

    return INNER * (at(1) - at(0)) + OUTER * (at(2) - at(-1))


def row_behind(ref, c, rows):
    def at(k):
        return ref[:, c, :, pl.ds(PAD + k, rows), :]

    return INNER * (at(0) - at(-1)) + OUTER * (at(1) - at(-2))


def pack_lanes(fields, lanes):
    slot_of = lanes // 4
    packed = jnp.zeros(lanes.shape, jnp.float32)
    k = 0
    for f in fields:
        for s in range(f.shape[0]):
            for z in range(f.shape[1]):
                packed = jnp.where(slot_of == k, turn(f[s, z], 4 * k + 2), packed)
                k += 1
    return packed


def lane_fix(own, left, right, lanes, per, ahead):
    place = lanes % 4
    kind = lanes // (4 * per)
    is_ahead = functools.reduce(
        jnp.logical_or, [kind == c for c, flag in enumerate(ahead) if flag]
    )

    def weight(ahead_at, behind_at):
        def table(entries):
            out = jnp.zeros(lanes.shape, jnp.float32)
            for j, value in entries:
                out = jnp.where(place == j, value, out)
            return out

        return jnp.where(is_ahead, table(ahead_at), table(behind_at))

    m = jnp.where(place < 2, left, right) - own
    return (
        weight([(0, OUTER), (1, OUTER)], []) * turn(m, -2)
        + weight([(1, INNER)], [(1, OUTER)]) * turn(m, -1)
        + weight([(2, -OUTER)], [(2, -INNER)]) * turn(m, 1)
        + weight([], [(2, -OUTER), (3, -OUTER)]) * turn(m, 2)
    )


def unpack_lanes(fix, first, count, depth, edge):
    parts = []
    for s in range(2):
        parts.append(
            jnp.stack(
                [
                    jnp.where(edge, turn(fix, -(4 * (first + s * depth + z) + 2)), 0.0)
                    for z in range(depth)
                ]
            )
        )
    return jnp.stack(parts)


def kernel(
    sizes,
    fwd,
    adj,
    lame_in,
    shear_in,
    buoy_in,
    mask_in,
    elem_in,
    table_in,
    new,
    mine,
    theirs,
    ext,
    rest,
    lame,
    shear,
    buoy,
    mask,
    elem,
    table,
    vext,
    sums,
    pack,
    from_left,
    from_right,
    load_sem,
    row_send,
    row_recv,
    lane_send,
    lane_recv,
    ev_send,
    ev_recv,
):
    n_ev, n_gx, n_gy = sizes
    ev, gx, gy = lax.axis_index("ev"), lax.axis_index("gx"), lax.axis_index("gy")
    _, _, depth, rows, cols = rest.shape
    per = 2 * depth

    barrier = pltpu.get_barrier_semaphore()
    has = {
        "up": gx > 0,
        "down": gx < n_gx - 1,
        "left": gy > 0,
        "right": gy < n_gy - 1,
    }
    where = {
        "up": {"gx": gx - 1},
        "down": {"gx": gx + 1},
        "left": {"gy": gy - 1},
        "right": {"gy": gy + 1},
    }
    mates = [{"ev": lax.rem(ev + d, n_ev)} for d in range(1, n_ev)]

    loads = {}

    def load(name, src, dst):
        copy = pltpu.make_async_copy(src, dst, load_sem.at[len(loads)])
        loads[name] = copy
        copy.start()

    for s, state in enumerate((fwd, adj)):
        load(("n0", s), state.at[0, pl.ds(3, 1)], ext.at[s, pl.ds(0, 1), :, pl.ds(PAD, rows), :])
        load(("n1", s), state.at[0, pl.ds(6, 2)], ext.at[s, pl.ds(1, 2), :, pl.ds(PAD, rows), :])
        load(("s0", s), state.at[0, pl.ds(4, 2)], rest.at[s, pl.ds(3, 2)])
        load(("s1", s), state.at[0, pl.ds(8, 1)], rest.at[s, pl.ds(5, 1)])
    for s, state in enumerate((fwd, adj)):
        load(("v", s), state.at[0, pl.ds(0, 3)], rest.at[s, pl.ds(0, 3)])
    load("table", table_in, table)
    load("elem", elem_in, elem)
    load("mask", mask_in, mask)
    load("buoy", buoy_in, buoy)
    load("lame", lame_in, lame)
    load("shear", shear_in, shear)

    for side in has:

        @pl.when(has[side])
        def _(side=side):
            pl.semaphore_signal(barrier, inc=1, device_id=where[side], device_id_type=MESH)

    for mate in mates:
        pl.semaphore_signal(barrier, inc=1, device_id=mate, device_id_type=MESH)

    @pl.when(gx == 0)
    def _():
        for ref in (ext, vext):
            ref[:, :, :, pl.ds(0, PAD), :] = jnp.zeros(ref.shape[:3] + (PAD, cols), jnp.float32)

    @pl.when(gx == n_gx - 1)
    def _():
        for ref in (ext, vext):
            ref[:, :, :, pl.ds(PAD + rows, PAD), :] = jnp.zeros(
                ref.shape[:3] + (PAD, cols), jnp.float32
            )

    @pl.when(gy == 0)
    def _():
        from_left[...] = jnp.zeros(from_left.shape, jnp.float32)

    @pl.when(gy == n_gy - 1)
    def _():
        from_right[...] = jnp.zeros(from_right.shape, jnp.float32)

    for s in range(2):
        for name in ("n0", "n1", "s0", "s1"):
            loads[name, s].wait()

    lanes = lax.broadcasted_iota(jnp.int32, (rows, cols), 1)
    edge = jnp.logical_or(lanes < 2, lanes >= cols - 2)

    def inside(ref, c):
        return ref[:, c, :, pl.ds(PAD, rows), :]

    def row_copy(ref, phase, side):
        start, goal = (PAD + rows - 2, PAD - 2) if side == "down" else (PAD, PAD + rows)
        i = 2 * phase + (side == "down")
        return pltpu.make_async_remote_copy(
            src_ref=ref.at[:, :, :, pl.ds(start, 2), :],
            dst_ref=ref.at[:, :, :, pl.ds(goal, 2), :],
            send_sem=row_send.at[i],
            recv_sem=row_recv.at[i],
            device_id=where[side],
            device_id_type=MESH,
        )

    def lane_copy(phase, side):
        i = 2 * phase + (side == "right")
        return pltpu.make_async_remote_copy(
            src_ref=pack.at[phase],
            dst_ref=(from_left if side == "right" else from_right).at[phase],
            send_sem=lane_send.at[i],
            recv_sem=lane_recv.at[i],
            device_id=where[side],
            device_id_type=MESH,
        )

    opposite = {"up": "down", "down": "up", "left": "right", "right": "left"}

    def copy_of(phase, side):
        if side in ("up", "down"):
            return row_copy((ext, vext)[phase], phase, side)
        return lane_copy(phase, side)

    def send(phase, sides):
        for side in sides:

            @pl.when(has[side])
            def _(side=side):
                copy_of(phase, side).start()

    def receive(phase, sides):
        for side in sides:

            @pl.when(has[side])
            def _(side=side):
                copy_of(phase, opposite[side]).wait_recv()

    def sent(phase):
        for side in has:

            @pl.when(has[side])
            def _(side=side):
                copy_of(phase, side).wait_send()

    sxy, syy, syz = inside(ext, 1), rest[:, 3], rest[:, 5]
    pack[0] = pack_lanes((sxy, syy, syz), lanes)

    peers = len(mates) + sum(flag.astype(jnp.int32) for flag in has.values())
    pl.semaphore_wait(barrier, peers)

    send(0, ("up", "down", "left", "right"))

    sums[0] = lane_ahead(sxy) + depth_ahead(inside(ext, 2))
    sums[1] = lane_behind(syy) + depth_ahead(syz)
    sums[2] = lane_ahead(syz) + depth_behind(rest[:, 4])

    for name in (("v", 0), ("v", 1), "table", "elem", "mask", "buoy"):
        loads[name].wait()
    entries = table.shape[2]
    chunks = [(a, min(a + cols, entries)) for a in range(0, entries, cols)]
    for z in range(depth):
        index = elem[z]
        gate = STEP * mask[z].astype(jnp.float32)
        low, high = index % cols, index // cols
        for i in range(3):
            value = jnp.zeros((rows, cols), jnp.float32)
            for j, (a, b) in enumerate(chunks):
                line = jnp.broadcast_to(table[i, :, pl.ds(a, b - a)], (rows, cols))
                value = jnp.where(high == j, jnp.take_along_axis(line, low, axis=1), value)
            rest[0, i, z] = rest[0, i, z] + gate * value

    receive(0, ("up", "down", "left", "right"))
    fix = lane_fix(pack[0], from_left[0], from_right[0], lanes, per, (True, False, True))
    force = buoy[...] * STEP
    force = jnp.stack([force, -force])
    row_diff = (row_behind, row_ahead, row_ahead)
    for i in range(3):
        divergence = (
            sums[i]
            + row_diff[i](ext, i, rows)
            + unpack_lanes(fix, i * per, per, depth, edge)
        )
        moved = rest[:, i] + force * divergence
        vext[:, i, :, pl.ds(PAD, rows), :] = moved
        new[0, i] = moved[0]

    velocity = [inside(vext, i) for i in range(3)]
    pack[1] = pack_lanes(velocity, lanes)
    send(1, ("up", "down", "left", "right"))

    def mate_copy(d, part):
        return pltpu.make_async_remote_copy(
            src_ref=mine.at[part],
            dst_ref=theirs.at[d, part],
            send_sem=ev_send.at[d, part],
            recv_sem=ev_recv.at[d, part],
            device_id=mates[d],
            device_id_type=MESH,
        )

    vx, vy, vz = velocity
    mine[2] = (
        vx[0] * (vx[1] - rest[1, 0]) + vy[0] * (vy[1] - rest[1, 1]) + vz[0] * (vz[1] - rest[1, 2])
    ) / STEP
    for d in range(len(mates)):
        mate_copy(d, 2).start()

    sums[0] = lane_behind(vx)
    sums[1] = lane_ahead(vy)
    sums[2] = lane_behind(vz) + depth_behind(vy)
    rate_z = depth_ahead(vz)
    shear_xz = depth_behind(vx)
    loads["lame"].wait()
    loads["shear"].wait()

    receive(1, ("up", "down", "left", "right"))
    fix = lane_fix(pack[1], from_left[1], from_right[1], lanes, per, (False, True, False))
    rate_x = row_ahead(vext, 0, rows)
    rate_y = sums[1] + unpack_lanes(fix, per, per, depth, edge)
    dilatation = rate_x + rate_y + rate_z
    mine[0] = dilatation[0] * dilatation[1]
    for d in range(len(mates)):
        mate_copy(d, 0).start()
    shear_xy = sums[0] + unpack_lanes(fix, 0, per, depth, edge) + row_behind(vext, 1, rows)
    shear_xz = shear_xz + row_behind(vext, 2, rows)
    shear_yz = sums[2] + unpack_lanes(fix, 2 * per, per, depth, edge)
    mine[1] = (
        2.0 * (rate_x[0] * rate_x[1] + rate_y[0] * rate_y[1] + rate_z[0] * rate_z[1])
        + shear_xy[0] * shear_xy[1]
        + shear_xz[0] * shear_xz[1]
        + shear_yz[0] * shear_yz[1]
    )
    for d in range(len(mates)):
        mate_copy(d, 1).start()

    mu = STEP * shear[...]
    bulk = STEP * lame[...] * dilatation[0]
    new[0, 3] = ext[0, 0, :, pl.ds(PAD, rows), :] + (bulk + 2.0 * mu * rate_x[0])
    new[0, 4] = rest[0, 3] + (bulk + 2.0 * mu * rate_y[0])
    new[0, 5] = rest[0, 4] + (bulk + 2.0 * mu * rate_z[0])
    new[0, 6] = ext[0, 1, :, pl.ds(PAD, rows), :] + mu * shear_xy[0]
    new[0, 7] = ext[0, 2, :, pl.ds(PAD, rows), :] + mu * shear_xz[0]
    new[0, 8] = rest[0, 5] + mu * shear_yz[0]
    for d in range(len(mates)):
        for part in (2, 0, 1):
            mate_copy(d, part).wait_recv()
    sent(0)
    sent(1)
    for d in range(len(mates)):
        for part in range(3):
            mate_copy(d, part).wait_send()


def finish(n_mates, new_in, mine, theirs, out, grad, total, sem):
    state_copy = pltpu.make_async_copy(new_in, out, sem.at[0])
    state_copy.start()
    value = mine[...]
    for d in range(n_mates):
        value = value + theirs[d]
    total[...] = value
    grad_copy = pltpu.make_async_copy(total, grad, sem.at[1])
    grad_copy.start()
    state_copy.wait()
    grad_copy.wait()


def solution(mesh):
    sizes = (mesh.shape["ev"], mesh.shape["gx"], mesh.shape["gy"])

    def shards(fwd, adj, lame, shear, buoy, mask, elem, table):
        _, _, depth, rows, cols = fwd.shape
        table = jnp.swapaxes(table, 0, 1)
        block = (depth, rows, cols)
        padded = (2, 3, depth, rows + 2 * PAD, cols)
        mates = max(sizes[0] - 1, 1)
        f32 = jnp.float32
        dma = pltpu.SemaphoreType.DMA
        anywhere = pl.BlockSpec(memory_space=pl.ANY)
        whole = pl.BlockSpec(memory_space=pltpu.VMEM)
        new, mine, theirs = pl.pallas_call(
            functools.partial(kernel, sizes),
            out_shape=(
                pltpu.VMEM(fwd.shape, f32),
                pltpu.VMEM((3,) + block, f32),
                pltpu.VMEM((mates, 3) + block, f32),
            ),
            in_specs=[anywhere] * 8,
            out_specs=(whole, whole, whole),
            scratch_shapes=[
                pltpu.VMEM(padded, f32),
                pltpu.VMEM((2, 6) + block, f32),
                pltpu.VMEM(block, f32),
                pltpu.VMEM(block, f32),
                pltpu.VMEM(block, f32),
                pltpu.VMEM(block, jnp.int32),
                pltpu.VMEM(block, jnp.int32),
                pltpu.VMEM(table.shape, f32),
                pltpu.VMEM(padded, f32),
                pltpu.VMEM((3, 2) + block, f32),
                pltpu.VMEM((2, rows, cols), f32),
                pltpu.VMEM((2, rows, cols), f32),
                pltpu.VMEM((2, rows, cols), f32),
                dma((16,)),
                dma((4,)),
                dma((4,)),
                dma((4,)),
                dma((4,)),
                dma((mates, 3)),
                dma((mates, 3)),
            ],
            compiler_params=pltpu.CompilerParams(
                collective_id=0, has_side_effects=True, vmem_limit_bytes=56 * 1024 * 1024
            ),
        )(fwd, adj, lame, shear, buoy, mask, elem, table)
        return pl.pallas_call(
            functools.partial(finish, sizes[0] - 1),
            out_shape=(
                jax.ShapeDtypeStruct(fwd.shape, f32),
                jax.ShapeDtypeStruct((3,) + block, f32),
            ),
            in_specs=[anywhere, whole, whole],
            out_specs=(anywhere, anywhere),
            scratch_shapes=[pltpu.VMEM((3,) + block, f32), dma((2,))],
            compiler_params=pltpu.CompilerParams(vmem_limit_bytes=8 * 1024 * 1024),
        )(new, mine, theirs)

    grid = P(None, "gx", "gy")
    state = P("ev", None, None, "gx", "gy")
    return jax.shard_map(
        shards,
        mesh=mesh,
        in_specs=(state, state, grid, grid, grid, grid, grid, P("ev", None, None)),
        out_specs=(state, P(None, None, "gx", "gy")),
        check_vma=False,
    )
```

```python
import functools

import jax
import jax.numpy as jnp
from jax import lax
from jax.experimental import pallas as pl
from jax.experimental.pallas import tpu as pltpu
from jax.sharding import PartitionSpec as P

MESH = pl.DeviceIdType.MESH
INNER = 9.0 / 8.0
OUTER = -1.0 / 24.0
STEP = 0.15
PAD = 8


def depth_ahead(f):
    zero = jnp.zeros_like(f[:, :1])
    p1 = jnp.concatenate([f[:, 1:], zero], 1)
    p2 = jnp.concatenate([f[:, 2:], zero, zero], 1)
    m1 = jnp.concatenate([zero, f[:, :-1]], 1)
    return INNER * (p1 - f) + OUTER * (p2 - m1)


def depth_behind(f):
    zero = jnp.zeros_like(f[:, :1])
    p1 = jnp.concatenate([f[:, 1:], zero], 1)
    m1 = jnp.concatenate([zero, f[:, :-1]], 1)
    m2 = jnp.concatenate([zero, zero, f[:, :-2]], 1)
    return INNER * (f - m1) + OUTER * (p1 - m2)


def turn(f, shift):
    return pltpu.roll(f, shift % f.shape[-1], f.ndim - 1)


def lane_ahead(f):
    return INNER * (turn(f, -1) - f) + OUTER * (turn(f, -2) - turn(f, 1))


def lane_behind(f):
    return INNER * (f - turn(f, 1)) + OUTER * (turn(f, -1) - turn(f, 2))


def row_ahead(ref, c, rows):
    def at(k):
        return ref[:, c, :, pl.ds(PAD + k, rows), :]

    return INNER * (at(1) - at(0)) + OUTER * (at(2) - at(-1))


def row_behind(ref, c, rows):
    def at(k):
        return ref[:, c, :, pl.ds(PAD + k, rows), :]

    return INNER * (at(0) - at(-1)) + OUTER * (at(1) - at(-2))


def pack_lanes(fields, lanes):
    slot_of = lanes // 4
    packed = jnp.zeros(lanes.shape, jnp.float32)
    k = 0
    for f in fields:
        for s in range(f.shape[0]):
            for z in range(f.shape[1]):
                packed = jnp.where(slot_of == k, turn(f[s, z], 4 * k + 2), packed)
                k += 1
    return packed


def lane_fix(own, left, right, lanes, per, ahead):
    place = lanes % 4
    kind = lanes // (4 * per)
    is_ahead = functools.reduce(
        jnp.logical_or, [kind == c for c, flag in enumerate(ahead) if flag]
    )

    def weight(ahead_at, behind_at):
        def table(entries):
            out = jnp.zeros(lanes.shape, jnp.float32)
            for j, value in entries:
                out = jnp.where(place == j, value, out)
            return out

        return jnp.where(is_ahead, table(ahead_at), table(behind_at))

    m = jnp.where(place < 2, left, right) - own
    return (
        weight([(0, OUTER), (1, OUTER)], []) * turn(m, -2)
        + weight([(1, INNER)], [(1, OUTER)]) * turn(m, -1)
        + weight([(2, -OUTER)], [(2, -INNER)]) * turn(m, 1)
        + weight([], [(2, -OUTER), (3, -OUTER)]) * turn(m, 2)
    )


def unpack_lanes(fix, first, count, depth, edge):
    parts = []
    for s in range(2):
        parts.append(
            jnp.stack(
                [
                    jnp.where(edge, turn(fix, -(4 * (first + s * depth + z) + 2)), 0.0)
                    for z in range(depth)
                ]
            )
        )
    return jnp.stack(parts)


def kernel(
    sizes,
    fwd,
    adj,
    lame_in,
    shear_in,
    buoy_in,
    mask_in,
    elem_in,
    table_in,
    new,
    mine,
    theirs,
    ext,
    rest,
    lame,
    shear,
    buoy,
    mask,
    elem,
    table,
    vext,
    sums,
    pack,
    from_left,
    from_right,
    load_sem,
    row_send,
    row_recv,
    lane_send,
    lane_recv,
    ev_send,
    ev_recv,
):
    n_ev, n_gx, n_gy = sizes
    ev, gx, gy = lax.axis_index("ev"), lax.axis_index("gx"), lax.axis_index("gy")
    _, _, depth, rows, cols = rest.shape
    per = 2 * depth

    barrier = pltpu.get_barrier_semaphore()
    has = {
        "up": gx > 0,
        "down": gx < n_gx - 1,
        "left": gy > 0,
        "right": gy < n_gy - 1,
    }
    where = {
        "up": {"gx": gx - 1},
        "down": {"gx": gx + 1},
        "left": {"gy": gy - 1},
        "right": {"gy": gy + 1},
    }
    mates = [{"ev": lax.rem(ev + d, n_ev)} for d in range(1, n_ev)]

    for side in has:

        @pl.when(has[side])
        def _(side=side):
            pl.semaphore_signal(barrier, inc=1, device_id=where[side], device_id_type=MESH)

    for mate in mates:
        pl.semaphore_signal(barrier, inc=1, device_id=mate, device_id_type=MESH)

    loads = {}

    def load(name, src, dst):
        copy = pltpu.make_async_copy(src, dst, load_sem.at[len(loads)])
        loads[name] = copy
        copy.start()

    for s, state in enumerate((fwd, adj)):
        load(("n0", s), state.at[0, pl.ds(3, 1)], ext.at[s, pl.ds(0, 1), :, pl.ds(PAD, rows), :])
        load(("n1", s), state.at[0, pl.ds(6, 2)], ext.at[s, pl.ds(1, 2), :, pl.ds(PAD, rows), :])
        load(("s0", s), state.at[0, pl.ds(4, 2)], rest.at[s, pl.ds(3, 2)])
        load(("s1", s), state.at[0, pl.ds(8, 1)], rest.at[s, pl.ds(5, 1)])
    for s, state in enumerate((fwd, adj)):
        load(("v", s), state.at[0, pl.ds(0, 3)], rest.at[s, pl.ds(0, 3)])
    load("table", table_in, table)
    load("elem", elem_in, elem)
    load("mask", mask_in, mask)
    load("buoy", buoy_in, buoy)
    load("lame", lame_in, lame)
    load("shear", shear_in, shear)

    @pl.when(gx == 0)
    def _():
        for ref in (ext, vext):
            ref[:, :, :, pl.ds(0, PAD), :] = jnp.zeros(ref.shape[:3] + (PAD, cols), jnp.float32)

    @pl.when(gx == n_gx - 1)
    def _():
        for ref in (ext, vext):
            ref[:, :, :, pl.ds(PAD + rows, PAD), :] = jnp.zeros(
                ref.shape[:3] + (PAD, cols), jnp.float32
            )

    @pl.when(gy == 0)
    def _():
        from_left[...] = jnp.zeros(from_left.shape, jnp.float32)

    @pl.when(gy == n_gy - 1)
    def _():
        from_right[...] = jnp.zeros(from_right.shape, jnp.float32)

    for s in range(2):
        for name in ("n0", "n1", "s0", "s1"):
            loads[name, s].wait()

    lanes = lax.broadcasted_iota(jnp.int32, (rows, cols), 1)
    edge = jnp.logical_or(lanes < 2, lanes >= cols - 2)

    def inside(ref, c):
        return ref[:, c, :, pl.ds(PAD, rows), :]

    def row_copy(ref, phase, side):
        start, goal = (PAD + rows - 2, PAD - 2) if side == "down" else (PAD, PAD + rows)
        i = 2 * phase + (side == "down")
        return pltpu.make_async_remote_copy(
            src_ref=ref.at[:, :, :, pl.ds(start, 2), :],
            dst_ref=ref.at[:, :, :, pl.ds(goal, 2), :],
            send_sem=row_send.at[i],
            recv_sem=row_recv.at[i],
            device_id=where[side],
            device_id_type=MESH,
        )

    def lane_copy(phase, side):
        i = 2 * phase + (side == "right")
        return pltpu.make_async_remote_copy(
            src_ref=pack.at[phase],
            dst_ref=(from_left if side == "right" else from_right).at[phase],
            send_sem=lane_send.at[i],
            recv_sem=lane_recv.at[i],
            device_id=where[side],
            device_id_type=MESH,
        )

    opposite = {"up": "down", "down": "up", "left": "right", "right": "left"}

    def copy_of(phase, side):
        if side in ("up", "down"):
            return row_copy((ext, vext)[phase], phase, side)
        return lane_copy(phase, side)

    def send(phase, sides):
        for side in sides:

            @pl.when(has[side])
            def _(side=side):
                copy_of(phase, side).start()

    def receive(phase, sides):
        for side in sides:

            @pl.when(has[side])
            def _(side=side):
                copy_of(phase, opposite[side]).wait_recv()

    def sent(phase):
        for side in has:

            @pl.when(has[side])
            def _(side=side):
                copy_of(phase, side).wait_send()

    sxy, syy, syz = inside(ext, 1), rest[:, 3], rest[:, 5]
    pack[0] = pack_lanes((sxy, syy, syz), lanes)

    peers = len(mates) + sum(flag.astype(jnp.int32) for flag in has.values())
    pl.semaphore_wait(barrier, peers)

    send(0, ("up", "down", "left", "right"))

    sums[0] = lane_ahead(sxy) + depth_ahead(inside(ext, 2))
    sums[1] = lane_behind(syy) + depth_ahead(syz)
    sums[2] = lane_ahead(syz) + depth_behind(rest[:, 4])

    for name in (("v", 0), ("v", 1), "table", "elem", "mask", "buoy"):
        loads[name].wait()
    entries = table.shape[2]
    chunks = [(a, min(a + cols, entries)) for a in range(0, entries, cols)]
    for z in range(depth):
        index = elem[z]
        gate = STEP * mask[z].astype(jnp.float32)
        low, high = index % cols, index // cols
        for i in range(3):
            value = jnp.zeros((rows, cols), jnp.float32)
            for j, (a, b) in enumerate(chunks):
                line = jnp.broadcast_to(table[i, :, pl.ds(a, b - a)], (rows, cols))
                value = jnp.where(high == j, jnp.take_along_axis(line, low, axis=1), value)
            rest[0, i, z] = rest[0, i, z] + gate * value

    receive(0, ("up", "down", "left", "right"))
    fix = lane_fix(pack[0], from_left[0], from_right[0], lanes, per, (True, False, True))
    force = buoy[...] * STEP
    force = jnp.stack([force, -force])
    row_diff = (row_behind, row_ahead, row_ahead)
    for i in range(3):
        divergence = (
            sums[i]
            + row_diff[i](ext, i, rows)
            + unpack_lanes(fix, i * per, per, depth, edge)
        )
        moved = rest[:, i] + force * divergence
        vext[:, i, :, pl.ds(PAD, rows), :] = moved
        new[0, i] = moved[0]

    velocity = [inside(vext, i) for i in range(3)]
    pack[1] = pack_lanes(velocity, lanes)
    send(1, ("up", "down", "left", "right"))

    def mate_copy(d, part):
        return pltpu.make_async_remote_copy(
            src_ref=mine.at[part],
            dst_ref=theirs.at[d, part],
            send_sem=ev_send.at[d, part],
            recv_sem=ev_recv.at[d, part],
            device_id=mates[d],
            device_id_type=MESH,
        )

    vx, vy, vz = velocity
    mine[2] = (
        vx[0] * (vx[1] - rest[1, 0]) + vy[0] * (vy[1] - rest[1, 1]) + vz[0] * (vz[1] - rest[1, 2])
    ) / STEP
    for d in range(len(mates)):
        mate_copy(d, 2).start()

    sums[0] = lane_behind(vx)
    sums[1] = lane_ahead(vy)
    sums[2] = lane_behind(vz) + depth_behind(vy)
    rate_z = depth_ahead(vz)
    shear_xz = depth_behind(vx)
    loads["lame"].wait()
    loads["shear"].wait()

    receive(1, ("up", "down", "left", "right"))
    fix = lane_fix(pack[1], from_left[1], from_right[1], lanes, per, (False, True, False))
    rate_x = row_ahead(vext, 0, rows)
    rate_y = sums[1] + unpack_lanes(fix, per, per, depth, edge)
    dilatation = rate_x + rate_y + rate_z
    mine[0] = dilatation[0] * dilatation[1]
    for d in range(len(mates)):
        mate_copy(d, 0).start()
    shear_xy = sums[0] + unpack_lanes(fix, 0, per, depth, edge) + row_behind(vext, 1, rows)
    shear_xz = shear_xz + row_behind(vext, 2, rows)
    shear_yz = sums[2] + unpack_lanes(fix, 2 * per, per, depth, edge)
    mine[1] = (
        2.0 * (rate_x[0] * rate_x[1] + rate_y[0] * rate_y[1] + rate_z[0] * rate_z[1])
        + shear_xy[0] * shear_xy[1]
        + shear_xz[0] * shear_xz[1]
        + shear_yz[0] * shear_yz[1]
    )
    for d in range(len(mates)):
        mate_copy(d, 1).start()

    mu = STEP * shear[...]
    bulk = STEP * lame[...] * dilatation[0]
    new[0, 3] = ext[0, 0, :, pl.ds(PAD, rows), :] + (bulk + 2.0 * mu * rate_x[0])
    new[0, 4] = rest[0, 3] + (bulk + 2.0 * mu * rate_y[0])
    new[0, 5] = rest[0, 4] + (bulk + 2.0 * mu * rate_z[0])
    new[0, 6] = ext[0, 1, :, pl.ds(PAD, rows), :] + mu * shear_xy[0]
    new[0, 7] = ext[0, 2, :, pl.ds(PAD, rows), :] + mu * shear_xz[0]
    new[0, 8] = rest[0, 5] + mu * shear_yz[0]
    for d in range(len(mates)):
        for part in (2, 0, 1):
            mate_copy(d, part).wait_recv()
    sent(0)
    sent(1)
    for d in range(len(mates)):
        for part in range(3):
            mate_copy(d, part).wait_send()


def finish(n_mates, new_in, mine, theirs, out, grad, total, sem):
    state_copy = pltpu.make_async_copy(new_in, out, sem.at[0])
    state_copy.start()
    value = mine[...]
    for d in range(n_mates):
        value = value + theirs[d]
    total[...] = value
    grad_copy = pltpu.make_async_copy(total, grad, sem.at[1])
    grad_copy.start()
    state_copy.wait()
    grad_copy.wait()


def solution(mesh):
    sizes = (mesh.shape["ev"], mesh.shape["gx"], mesh.shape["gy"])

    def shards(fwd, adj, lame, shear, buoy, mask, elem, table):
        _, _, depth, rows, cols = fwd.shape
        table = jnp.swapaxes(table, 0, 1)
        block = (depth, rows, cols)
        padded = (2, 3, depth, rows + 2 * PAD, cols)
        mates = max(sizes[0] - 1, 1)
        f32 = jnp.float32
        dma = pltpu.SemaphoreType.DMA
        anywhere = pl.BlockSpec(memory_space=pl.ANY)
        whole = pl.BlockSpec(memory_space=pltpu.VMEM)
        new, mine, theirs = pl.pallas_call(
            functools.partial(kernel, sizes),
            out_shape=(
                pltpu.VMEM(fwd.shape, f32),
                pltpu.VMEM((3,) + block, f32),
                pltpu.VMEM((mates, 3) + block, f32),
            ),
            in_specs=[anywhere] * 8,
            out_specs=(whole, whole, whole),
            scratch_shapes=[
                pltpu.VMEM(padded, f32),
                pltpu.VMEM((2, 6) + block, f32),
                pltpu.VMEM(block, f32),
                pltpu.VMEM(block, f32),
                pltpu.VMEM(block, f32),
                pltpu.VMEM(block, jnp.int32),
                pltpu.VMEM(block, jnp.int32),
                pltpu.VMEM(table.shape, f32),
                pltpu.VMEM(padded, f32),
                pltpu.VMEM((3, 2) + block, f32),
                pltpu.VMEM((2, rows, cols), f32),
                pltpu.VMEM((2, rows, cols), f32),
                pltpu.VMEM((2, rows, cols), f32),
                dma((16,)),
                dma((4,)),
                dma((4,)),
                dma((4,)),
                dma((4,)),
                dma((mates, 3)),
                dma((mates, 3)),
            ],
            compiler_params=pltpu.CompilerParams(
                collective_id=0, has_side_effects=True, vmem_limit_bytes=56 * 1024 * 1024
            ),
        )(fwd, adj, lame, shear, buoy, mask, elem, table)
        return pl.pallas_call(
            functools.partial(finish, sizes[0] - 1),
            out_shape=(
                jax.ShapeDtypeStruct(fwd.shape, f32),
                jax.ShapeDtypeStruct((3,) + block, f32),
            ),
            in_specs=[anywhere, whole, whole],
            out_specs=(anywhere, anywhere),
            scratch_shapes=[pltpu.VMEM((3,) + block, f32), dma((2,))],
            compiler_params=pltpu.CompilerParams(vmem_limit_bytes=8 * 1024 * 1024),
        )(new, mine, theirs)

    grid = P(None, "gx", "gy")
    state = P("ev", None, None, "gx", "gy")
    return jax.shard_map(
        shards,
        mesh=mesh,
        in_specs=(state, state, grid, grid, grid, grid, grid, P("ev", None, None)),
        out_specs=(state, P(None, None, "gx", "gy")),
        check_vma=False,
    )
```

```python
import functools

import jax
import jax.numpy as jnp
from jax import lax
from jax.experimental import pallas as pl
from jax.experimental.pallas import tpu as pltpu
from jax.sharding import PartitionSpec as P

MESH = pl.DeviceIdType.MESH
INNER = 9.0 / 8.0
OUTER = -1.0 / 24.0
STEP = 0.15
PAD = 8


def depth_ahead(f):
    zero = jnp.zeros_like(f[:, :1])
    p1 = jnp.concatenate([f[:, 1:], zero], 1)
    p2 = jnp.concatenate([f[:, 2:], zero, zero], 1)
    m1 = jnp.concatenate([zero, f[:, :-1]], 1)
    return INNER * (p1 - f) + OUTER * (p2 - m1)


def depth_behind(f):
    zero = jnp.zeros_like(f[:, :1])
    p1 = jnp.concatenate([f[:, 1:], zero], 1)
    m1 = jnp.concatenate([zero, f[:, :-1]], 1)
    m2 = jnp.concatenate([zero, zero, f[:, :-2]], 1)
    return INNER * (f - m1) + OUTER * (p1 - m2)


def turn(f, shift):
    return pltpu.roll(f, shift % f.shape[-1], f.ndim - 1)


def lane_ahead(f):
    return INNER * (turn(f, -1) - f) + OUTER * (turn(f, -2) - turn(f, 1))


def lane_behind(f):
    return INNER * (f - turn(f, 1)) + OUTER * (turn(f, -1) - turn(f, 2))


def row_ahead(ref, c, rows):
    def at(k):
        return ref[:, c, :, pl.ds(PAD + k, rows), :]

    return INNER * (at(1) - at(0)) + OUTER * (at(2) - at(-1))


def row_behind(ref, c, rows):
    def at(k):
        return ref[:, c, :, pl.ds(PAD + k, rows), :]

    return INNER * (at(0) - at(-1)) + OUTER * (at(1) - at(-2))


def pack_lanes(fields, lanes):
    slot_of = lanes // 4
    packed = jnp.zeros(lanes.shape, jnp.float32)
    k = 0
    for f in fields:
        for s in range(f.shape[0]):
            for z in range(f.shape[1]):
                packed = jnp.where(slot_of == k, turn(f[s, z], 4 * k + 2), packed)
                k += 1
    return packed


def lane_fix(own, left, right, lanes, per, ahead):
    place = lanes % 4
    kind = lanes // (4 * per)
    is_ahead = functools.reduce(
        jnp.logical_or, [kind == c for c, flag in enumerate(ahead) if flag]
    )

    def weight(ahead_at, behind_at):
        def table(entries):
            out = jnp.zeros(lanes.shape, jnp.float32)
            for j, value in entries:
                out = jnp.where(place == j, value, out)
            return out

        return jnp.where(is_ahead, table(ahead_at), table(behind_at))

    m = jnp.where(place < 2, left, right) - own
    return (
        weight([(0, OUTER), (1, OUTER)], []) * turn(m, -2)
        + weight([(1, INNER)], [(1, OUTER)]) * turn(m, -1)
        + weight([(2, -OUTER)], [(2, -INNER)]) * turn(m, 1)
        + weight([], [(2, -OUTER), (3, -OUTER)]) * turn(m, 2)
    )


def unpack_lanes(fix, first, count, depth, edge):
    parts = []
    for s in range(2):
        parts.append(
            jnp.stack(
                [
                    jnp.where(edge, turn(fix, -(4 * (first + s * depth + z) + 2)), 0.0)
                    for z in range(depth)
                ]
            )
        )
    return jnp.stack(parts)


def kernel(
    sizes,
    fwd,
    adj,
    lame_in,
    shear_in,
    buoy_in,
    mask_in,
    elem_in,
    table_in,
    new,
    mine,
    theirs,
    theirs_rows,
    theirs_lanes,
    ext,
    rest,
    lame,
    shear,
    buoy,
    mask,
    elem,
    table,
    vext,
    sums,
    pack,
    from_left,
    from_right,
    vint,
    early,
    mine_lanes,
    load_sem,
    row_send,
    row_recv,
    lane_send,
    lane_recv,
    ev_send,
    ev_recv,
):
    n_ev, n_gx, n_gy = sizes
    ev, gx, gy = lax.axis_index("ev"), lax.axis_index("gx"), lax.axis_index("gy")
    _, _, depth, rows, cols = rest.shape
    per = 2 * depth

    barrier = pltpu.get_barrier_semaphore()
    has = {
        "up": gx > 0,
        "down": gx < n_gx - 1,
        "left": gy > 0,
        "right": gy < n_gy - 1,
    }
    where = {
        "up": {"gx": gx - 1},
        "down": {"gx": gx + 1},
        "left": {"gy": gy - 1},
        "right": {"gy": gy + 1},
    }
    mates = [{"ev": lax.rem(ev + d, n_ev)} for d in range(1, n_ev)]

    for side in has:

        @pl.when(has[side])
        def _(side=side):
            pl.semaphore_signal(barrier, inc=1, device_id=where[side], device_id_type=MESH)

    for mate in mates:
        pl.semaphore_signal(barrier, inc=1, device_id=mate, device_id_type=MESH)

    loads = {}

    def load(name, src, dst):
        copy = pltpu.make_async_copy(src, dst, load_sem.at[len(loads)])
        loads[name] = copy
        copy.start()

    for s, state in enumerate((fwd, adj)):
        load(("n0", s), state.at[0, pl.ds(3, 1)], ext.at[s, pl.ds(0, 1), :, pl.ds(PAD, rows), :])
        load(("n1", s), state.at[0, pl.ds(6, 2)], ext.at[s, pl.ds(1, 2), :, pl.ds(PAD, rows), :])
        load(("s0", s), state.at[0, pl.ds(4, 2)], rest.at[s, pl.ds(3, 2)])
        load(("s1", s), state.at[0, pl.ds(8, 1)], rest.at[s, pl.ds(5, 1)])
    for s, state in enumerate((fwd, adj)):
        load(("v", s), state.at[0, pl.ds(0, 3)], rest.at[s, pl.ds(0, 3)])
    load("table", table_in, table)
    load("elem", elem_in, elem)
    load("mask", mask_in, mask)
    load("buoy", buoy_in, buoy)
    load("lame", lame_in, lame)
    load("shear", shear_in, shear)

    for start in (0, PAD + rows):
        vint[:, :, :, pl.ds(start, PAD), :] = jnp.zeros(vint.shape[:3] + (PAD, cols), jnp.float32)

    @pl.when(gx == 0)
    def _():
        for ref in (ext, vext):
            ref[:, :, :, pl.ds(0, PAD), :] = jnp.zeros(ref.shape[:3] + (PAD, cols), jnp.float32)

    @pl.when(gx == n_gx - 1)
    def _():
        for ref in (ext, vext):
            ref[:, :, :, pl.ds(PAD + rows, PAD), :] = jnp.zeros(
                ref.shape[:3] + (PAD, cols), jnp.float32
            )

    @pl.when(gy == 0)
    def _():
        from_left[...] = jnp.zeros(from_left.shape, jnp.float32)

    @pl.when(gy == n_gy - 1)
    def _():
        from_right[...] = jnp.zeros(from_right.shape, jnp.float32)

    for s in range(2):
        for name in ("n0", "n1", "s0", "s1"):
            loads[name, s].wait()

    lanes = lax.broadcasted_iota(jnp.int32, (rows, cols), 1)
    edge = jnp.logical_or(lanes < 2, lanes >= cols - 2)

    def inside(ref, c):
        return ref[:, c, :, pl.ds(PAD, rows), :]

    def row_copy(ref, phase, side):
        start, goal = (PAD + rows - 2, PAD - 2) if side == "down" else (PAD, PAD + rows)
        i = 2 * phase + (side == "down")
        return pltpu.make_async_remote_copy(
            src_ref=ref.at[:, :, :, pl.ds(start, 2), :],
            dst_ref=ref.at[:, :, :, pl.ds(goal, 2), :],
            send_sem=row_send.at[i],
            recv_sem=row_recv.at[i],
            device_id=where[side],
            device_id_type=MESH,
        )

    def lane_copy(phase, side):
        i = 2 * phase + (side == "right")
        return pltpu.make_async_remote_copy(
            src_ref=pack.at[phase],
            dst_ref=(from_left if side == "right" else from_right).at[phase],
            send_sem=lane_send.at[i],
            recv_sem=lane_recv.at[i],
            device_id=where[side],
            device_id_type=MESH,
        )

    opposite = {"up": "down", "down": "up", "left": "right", "right": "left"}

    def copy_of(phase, side):
        if side in ("up", "down"):
            return row_copy((ext, vext)[phase], phase, side)
        return lane_copy(phase, side)

    def send(phase, sides):
        for side in sides:

            @pl.when(has[side])
            def _(side=side):
                copy_of(phase, side).start()

    def receive(phase, sides):
        for side in sides:

            @pl.when(has[side])
            def _(side=side):
                copy_of(phase, opposite[side]).wait_recv()

    def sent(phase):
        for side in has:

            @pl.when(has[side])
            def _(side=side):
                copy_of(phase, side).wait_send()

    sxy, syy, syz = inside(ext, 1), rest[:, 3], rest[:, 5]
    pack[0] = pack_lanes((sxy, syy, syz), lanes)

    peers = len(mates) + sum(flag.astype(jnp.int32) for flag in has.values())
    pl.semaphore_wait(barrier, peers)

    send(0, ("up", "down", "left", "right"))

    sums[0] = lane_ahead(sxy) + depth_ahead(inside(ext, 2))
    sums[1] = lane_behind(syy) + depth_ahead(syz)
    sums[2] = lane_ahead(syz) + depth_behind(rest[:, 4])

    for name in (("v", 0), ("v", 1), "table", "elem", "mask", "buoy"):
        loads[name].wait()
    entries = table.shape[2]
    chunks = [(a, min(a + cols, entries)) for a in range(0, entries, cols)]
    for z in range(depth):
        index = elem[z]
        gate = STEP * mask[z].astype(jnp.float32)
        low, high = index % cols, index // cols
        for i in range(3):
            value = jnp.zeros((rows, cols), jnp.float32)
            for j, (a, b) in enumerate(chunks):
                line = jnp.broadcast_to(table[i, :, pl.ds(a, b - a)], (rows, cols))
                value = jnp.where(high == j, jnp.take_along_axis(line, low, axis=1), value)
            rest[0, i, z] = rest[0, i, z] + gate * value

    receive(0, ("up", "down", "left", "right"))
    fix = lane_fix(pack[0], from_left[0], from_right[0], lanes, per, (True, False, True))
    force = buoy[...] * STEP
    force = jnp.stack([force, -force])
    row_diff = (row_behind, row_ahead, row_ahead)
    for i in range(3):
        divergence = (
            sums[i]
            + row_diff[i](ext, i, rows)
            + unpack_lanes(fix, i * per, per, depth, edge)
        )
        moved = rest[:, i] + force * divergence
        vext[:, i, :, pl.ds(PAD, rows), :] = moved
        new[0, i] = moved[0]

    velocity = [inside(vext, i) for i in range(3)]
    pack[1] = pack_lanes(velocity, lanes)
    send(1, ("up", "down", "left", "right"))

    def mate_copy(d, part):
        top, bottom = pl.ds(0, 2), pl.ds(rows - 2, 2)
        both = pl.ds(0, 2)
        src, dst = (
            (mine.at[2], theirs.at[d, 2]),
            (early, theirs.at[d, both]),
            (mine.at[both, :, top, :], theirs_rows.at[d, :, :, top, :]),
            (mine.at[both, :, bottom, :], theirs_rows.at[d, :, :, bottom, :]),
            (mine_lanes, theirs_lanes.at[d]),
        )[part]
        return pltpu.make_async_remote_copy(
            src_ref=src,
            dst_ref=dst,
            send_sem=ev_send.at[d, part],
            recv_sem=ev_recv.at[d, part],
            device_id=mates[d],
            device_id_type=MESH,
        )

    def to_mates(*parts):
        for d in range(len(mates)):
            for part in parts:
                mate_copy(d, part).start()

    def terms(rate_x, rate_y, rate_z, shear_xy, shear_xz, shear_yz):
        dilatation = rate_x + rate_y + rate_z
        modulus = (
            2.0 * (rate_x[0] * rate_x[1] + rate_y[0] * rate_y[1] + rate_z[0] * rate_z[1])
            + shear_xy[0] * shear_xy[1]
            + shear_xz[0] * shear_xz[1]
            + shear_yz[0] * shear_yz[1]
        )
        return dilatation, dilatation[0] * dilatation[1], modulus

    vx, vy, vz = velocity
    mine[2] = (
        vx[0] * (vx[1] - rest[1, 0]) + vy[0] * (vy[1] - rest[1, 1]) + vz[0] * (vz[1] - rest[1, 2])
    ) / STEP
    to_mates(0)

    sums[0] = lane_behind(vx)
    sums[1] = lane_ahead(vy)
    sums[2] = lane_behind(vz) + depth_behind(vy)
    rate_z = depth_ahead(vz)
    shear_xz = depth_behind(vx)

    for i in range(3):
        vint[:, i, :, pl.ds(PAD, rows), :] = velocity[i]
    _, early[0], early[1] = terms(
        row_ahead(vint, 0, rows),
        sums[1],
        rate_z,
        sums[0] + row_behind(vint, 1, rows),
        shear_xz + row_behind(vint, 2, rows),
        sums[2],
    )
    to_mates(1)
    loads["lame"].wait()
    loads["shear"].wait()

    receive(1, ("up", "down", "left", "right"))
    fix = lane_fix(pack[1], from_left[1], from_right[1], lanes, per, (False, True, False))
    rate_x = row_ahead(vext, 0, rows)
    rate_y = sums[1] + unpack_lanes(fix, per, per, depth, edge)
    shear_xy = sums[0] + unpack_lanes(fix, 0, per, depth, edge) + row_behind(vext, 1, rows)
    shear_xz = shear_xz + row_behind(vext, 2, rows)
    shear_yz = sums[2] + unpack_lanes(fix, 2 * per, per, depth, edge)
    dilatation, mine[0], mine[1] = terms(rate_x, rate_y, rate_z, shear_xy, shear_xz, shear_yz)
    to_mates(2, 3)
    mine_lanes[...] = pack_lanes((mine[pl.ds(0, 2)],), lanes)
    to_mates(4)

    mu = STEP * shear[...]
    bulk = STEP * lame[...] * dilatation[0]
    new[0, 3] = ext[0, 0, :, pl.ds(PAD, rows), :] + (bulk + 2.0 * mu * rate_x[0])
    new[0, 4] = rest[0, 3] + (bulk + 2.0 * mu * rate_y[0])
    new[0, 5] = rest[0, 4] + (bulk + 2.0 * mu * rate_z[0])
    new[0, 6] = ext[0, 1, :, pl.ds(PAD, rows), :] + mu * shear_xy[0]
    new[0, 7] = ext[0, 2, :, pl.ds(PAD, rows), :] + mu * shear_xz[0]
    new[0, 8] = rest[0, 5] + mu * shear_yz[0]
    for d in range(len(mates)):
        for part in range(5):
            mate_copy(d, part).wait_recv()
    sent(0)
    sent(1)
    for d in range(len(mates)):
        for part in range(5):
            mate_copy(d, part).wait_send()


def finish(n_mates, new_in, mine, theirs, theirs_rows, theirs_lanes, out, grad, total, sem):
    state_copy = pltpu.make_async_copy(new_in, out, sem.at[0])
    state_copy.start()
    _, depth, rows, cols = mine.shape
    lanes = lax.broadcasted_iota(jnp.int32, (rows, cols), 1)
    edge = jnp.logical_or(lanes < 2, lanes >= cols - 2)
    for part in range(3):
        for z in range(depth):
            value = mine[part, z]
            for d in range(n_mates):
                other = theirs[d, part, z]
                if part < 2:
                    last = turn(theirs_lanes[d], -(4 * (part * depth + z) + 2))
                    other = jnp.where(edge, last, other)
                value = value + other
            total[part, z] = value
    if n_mates:
        for start in (0, rows - 2):
            ends = pl.ds(start, 2)
            value = mine[pl.ds(0, 2), :, ends, :]
            for d in range(n_mates):
                value = value + theirs_rows[d, :, :, ends, :]
            total[pl.ds(0, 2), :, ends, :] = value
    grad_copy = pltpu.make_async_copy(total, grad, sem.at[1])
    grad_copy.start()
    state_copy.wait()
    grad_copy.wait()


def solution(mesh):
    sizes = (mesh.shape["ev"], mesh.shape["gx"], mesh.shape["gy"])

    def shards(fwd, adj, lame, shear, buoy, mask, elem, table):
        _, _, depth, rows, cols = fwd.shape
        table = jnp.swapaxes(table, 0, 1)
        block = (depth, rows, cols)
        padded = (2, 3, depth, rows + 2 * PAD, cols)
        mates = max(sizes[0] - 1, 1)
        f32 = jnp.float32
        dma = pltpu.SemaphoreType.DMA
        anywhere = pl.BlockSpec(memory_space=pl.ANY)
        whole = pl.BlockSpec(memory_space=pltpu.VMEM)
        new, *pieces = pl.pallas_call(
            functools.partial(kernel, sizes),
            out_shape=(
                pltpu.VMEM(fwd.shape, f32),
                pltpu.VMEM((3,) + block, f32),
                pltpu.VMEM((mates, 3) + block, f32),
                pltpu.VMEM((mates, 2) + block, f32),
                pltpu.VMEM((mates, rows, cols), f32),
            ),
            in_specs=[anywhere] * 8,
            out_specs=(whole,) * 5,
            scratch_shapes=[
                pltpu.VMEM(padded, f32),
                pltpu.VMEM((2, 6) + block, f32),
                pltpu.VMEM(block, f32),
                pltpu.VMEM(block, f32),
                pltpu.VMEM(block, f32),
                pltpu.VMEM(block, jnp.int32),
                pltpu.VMEM(block, jnp.int32),
                pltpu.VMEM(table.shape, f32),
                pltpu.VMEM(padded, f32),
                pltpu.VMEM((3, 2) + block, f32),
                pltpu.VMEM((2, rows, cols), f32),
                pltpu.VMEM((2, rows, cols), f32),
                pltpu.VMEM((2, rows, cols), f32),
                pltpu.VMEM(padded, f32),
                pltpu.VMEM((2,) + block, f32),
                pltpu.VMEM((rows, cols), f32),
                dma((16,)),
                dma((4,)),
                dma((4,)),
                dma((4,)),
                dma((4,)),
                dma((mates, 5)),
                dma((mates, 5)),
            ],
            compiler_params=pltpu.CompilerParams(
                collective_id=0, has_side_effects=True, vmem_limit_bytes=56 * 1024 * 1024
            ),
        )(fwd, adj, lame, shear, buoy, mask, elem, table)
        return pl.pallas_call(
            functools.partial(finish, sizes[0] - 1),
            out_shape=(
                jax.ShapeDtypeStruct(fwd.shape, f32),
                jax.ShapeDtypeStruct((3,) + block, f32),
            ),
            in_specs=[anywhere] + [whole] * 4,
            out_specs=(anywhere, anywhere),
            scratch_shapes=[pltpu.VMEM((3,) + block, f32), dma((2,))],
            compiler_params=pltpu.CompilerParams(vmem_limit_bytes=8 * 1024 * 1024),
        )(new, *pieces)

    grid = P(None, "gx", "gy")
    state = P("ev", None, None, "gx", "gy")
    return jax.shard_map(
        shards,
        mesh=mesh,
        in_specs=(state, state, grid, grid, grid, grid, grid, P("ev", None, None)),
        out_specs=(state, P(None, None, "gx", "gy")),
        check_vma=False,
    )
```

```python
import functools

import jax
import jax.numpy as jnp
from jax import lax
from jax.experimental import pallas as pl
from jax.experimental.pallas import tpu as pltpu
from jax.sharding import PartitionSpec as P

MESH = pl.DeviceIdType.MESH
INNER = 9.0 / 8.0
OUTER = -1.0 / 24.0
STEP = 0.15
PAD = 8


def depth_ahead(f):
    zero = jnp.zeros_like(f[:, :1])
    p1 = jnp.concatenate([f[:, 1:], zero], 1)
    p2 = jnp.concatenate([f[:, 2:], zero, zero], 1)
    m1 = jnp.concatenate([zero, f[:, :-1]], 1)
    return INNER * (p1 - f) + OUTER * (p2 - m1)


def depth_behind(f):
    zero = jnp.zeros_like(f[:, :1])
    p1 = jnp.concatenate([f[:, 1:], zero], 1)
    m1 = jnp.concatenate([zero, f[:, :-1]], 1)
    m2 = jnp.concatenate([zero, zero, f[:, :-2]], 1)
    return INNER * (f - m1) + OUTER * (p1 - m2)


def turn(f, shift):
    return pltpu.roll(f, shift % f.shape[-1], f.ndim - 1)


def lane_ahead(f):
    return INNER * (turn(f, -1) - f) + OUTER * (turn(f, -2) - turn(f, 1))


def lane_behind(f):
    return INNER * (f - turn(f, 1)) + OUTER * (turn(f, -1) - turn(f, 2))


def row_ahead(ref, c, rows, first=0):
    def at(k):
        return ref[:, c, :, pl.ds(PAD + first + k, rows), :]

    return INNER * (at(1) - at(0)) + OUTER * (at(2) - at(-1))


def row_behind(ref, c, rows, first=0):
    def at(k):
        return ref[:, c, :, pl.ds(PAD + first + k, rows), :]

    return INNER * (at(0) - at(-1)) + OUTER * (at(1) - at(-2))


def pack_lanes(fields, lanes):
    slot_of = lanes // 4
    packed = jnp.zeros(lanes.shape, jnp.float32)
    k = 0
    for f in fields:
        for s in range(f.shape[0]):
            for z in range(f.shape[1]):
                packed = jnp.where(slot_of == k, turn(f[s, z], 4 * k + 2), packed)
                k += 1
    return packed


def lane_fix(own, left, right, lanes, per, ahead):
    place = lanes % 4
    kind = lanes // (4 * per)
    is_ahead = functools.reduce(
        jnp.logical_or, [kind == c for c, flag in enumerate(ahead) if flag]
    )

    def weight(ahead_at, behind_at):
        def table(entries):
            out = jnp.zeros(lanes.shape, jnp.float32)
            for j, value in entries:
                out = jnp.where(place == j, value, out)
            return out

        return jnp.where(is_ahead, table(ahead_at), table(behind_at))

    m = jnp.where(place < 2, left, right) - own
    return (
        weight([(0, OUTER), (1, OUTER)], []) * turn(m, -2)
        + weight([(1, INNER)], [(1, OUTER)]) * turn(m, -1)
        + weight([(2, -OUTER)], [(2, -INNER)]) * turn(m, 1)
        + weight([], [(2, -OUTER), (3, -OUTER)]) * turn(m, 2)
    )


def unpack_lanes(fix, first, count, depth, edge):
    parts = []
    for s in range(2):
        parts.append(
            jnp.stack(
                [
                    jnp.where(edge, turn(fix, -(4 * (first + s * depth + z) + 2)), 0.0)
                    for z in range(depth)
                ]
            )
        )
    return jnp.stack(parts)


def kernel(
    sizes,
    fwd,
    adj,
    lame_in,
    shear_in,
    buoy_in,
    mask_in,
    elem_in,
    table_in,
    new,
    mine,
    theirs,
    theirs_lanes,
    ext,
    rest,
    lame,
    shear,
    buoy,
    mask,
    elem,
    table,
    vext,
    sums,
    pack,
    from_left,
    from_right,
    vint,
    early,
    mine_lanes,
    load_sem,
    row_send,
    row_recv,
    lane_send,
    lane_recv,
    ev_send,
    ev_recv,
):
    n_ev, n_gx, n_gy = sizes
    ev, gx, gy = lax.axis_index("ev"), lax.axis_index("gx"), lax.axis_index("gy")
    _, _, depth, rows, cols = rest.shape
    per = 2 * depth

    barrier = pltpu.get_barrier_semaphore()
    has = {
        "up": gx > 0,
        "down": gx < n_gx - 1,
        "left": gy > 0,
        "right": gy < n_gy - 1,
    }
    where = {
        "up": {"gx": gx - 1},
        "down": {"gx": gx + 1},
        "left": {"gy": gy - 1},
        "right": {"gy": gy + 1},
    }
    mates = [{"ev": lax.rem(ev + d, n_ev)} for d in range(1, n_ev)]

    for side in has:

        @pl.when(has[side])
        def _(side=side):
            pl.semaphore_signal(barrier, inc=1, device_id=where[side], device_id_type=MESH)

    for mate in mates:
        pl.semaphore_signal(barrier, inc=1, device_id=mate, device_id_type=MESH)

    loads = {}

    def load(name, src, dst):
        copy = pltpu.make_async_copy(src, dst, load_sem.at[len(loads)])
        loads[name] = copy
        copy.start()

    for s, state in enumerate((fwd, adj)):
        load(("n0", s), state.at[0, pl.ds(3, 1)], ext.at[s, pl.ds(0, 1), :, pl.ds(PAD, rows), :])
        load(("n1", s), state.at[0, pl.ds(6, 2)], ext.at[s, pl.ds(1, 2), :, pl.ds(PAD, rows), :])
        load(("s0", s), state.at[0, pl.ds(4, 2)], rest.at[s, pl.ds(3, 2)])
        load(("s1", s), state.at[0, pl.ds(8, 1)], rest.at[s, pl.ds(5, 1)])
    for s, state in enumerate((fwd, adj)):
        load(("v", s), state.at[0, pl.ds(0, 3)], rest.at[s, pl.ds(0, 3)])
    load("table", table_in, table)
    load("elem", elem_in, elem)
    load("mask", mask_in, mask)
    load("buoy", buoy_in, buoy)
    load("lame", lame_in, lame)
    load("shear", shear_in, shear)

    for start in (0, PAD + rows):
        vint[:, :, :, pl.ds(start, PAD), :] = jnp.zeros(vint.shape[:3] + (PAD, cols), jnp.float32)

    @pl.when(gx == 0)
    def _():
        for ref in (ext, vext):
            ref[:, :, :, pl.ds(0, PAD), :] = jnp.zeros(ref.shape[:3] + (PAD, cols), jnp.float32)

    @pl.when(gx == n_gx - 1)
    def _():
        for ref in (ext, vext):
            ref[:, :, :, pl.ds(PAD + rows, PAD), :] = jnp.zeros(
                ref.shape[:3] + (PAD, cols), jnp.float32
            )

    @pl.when(gy == 0)
    def _():
        from_left[...] = jnp.zeros(from_left.shape, jnp.float32)

    @pl.when(gy == n_gy - 1)
    def _():
        from_right[...] = jnp.zeros(from_right.shape, jnp.float32)

    for s in range(2):
        for name in ("n0", "n1", "s0", "s1"):
            loads[name, s].wait()

    lanes = lax.broadcasted_iota(jnp.int32, (rows, cols), 1)
    edge = jnp.logical_or(lanes < 2, lanes >= cols - 2)

    def inside(ref, c):
        return ref[:, c, :, pl.ds(PAD, rows), :]

    def row_copy(ref, phase, side):
        start, goal = (PAD + rows - 2, PAD - 2) if side == "down" else (PAD, PAD + rows)
        i = 2 * phase + (side == "down")
        return pltpu.make_async_remote_copy(
            src_ref=ref.at[:, :, :, pl.ds(start, 2), :],
            dst_ref=ref.at[:, :, :, pl.ds(goal, 2), :],
            send_sem=row_send.at[i],
            recv_sem=row_recv.at[i],
            device_id=where[side],
            device_id_type=MESH,
        )

    def lane_copy(phase, side):
        i = 2 * phase + (side == "right")
        return pltpu.make_async_remote_copy(
            src_ref=pack.at[phase],
            dst_ref=(from_left if side == "right" else from_right).at[phase],
            send_sem=lane_send.at[i],
            recv_sem=lane_recv.at[i],
            device_id=where[side],
            device_id_type=MESH,
        )

    opposite = {"up": "down", "down": "up", "left": "right", "right": "left"}

    def copy_of(phase, side):
        if side in ("up", "down"):
            return row_copy((ext, vext)[phase], phase, side)
        return lane_copy(phase, side)

    def send(phase, sides):
        for side in sides:

            @pl.when(has[side])
            def _(side=side):
                copy_of(phase, side).start()

    def receive(phase, sides):
        for side in sides:

            @pl.when(has[side])
            def _(side=side):
                copy_of(phase, opposite[side]).wait_recv()

    def sent(phase):
        for side in has:

            @pl.when(has[side])
            def _(side=side):
                copy_of(phase, side).wait_send()

    sxy, syy, syz = inside(ext, 1), rest[:, 3], rest[:, 5]
    pack[0] = pack_lanes((sxy, syy, syz), lanes)

    peers = len(mates) + sum(flag.astype(jnp.int32) for flag in has.values())
    pl.semaphore_wait(barrier, peers)

    send(0, ("up", "down", "left", "right"))

    sums[0] = lane_ahead(sxy) + depth_ahead(inside(ext, 2))
    sums[1] = lane_behind(syy) + depth_ahead(syz)
    sums[2] = lane_ahead(syz) + depth_behind(rest[:, 4])

    for name in (("v", 0), ("v", 1), "table", "elem", "mask", "buoy"):
        loads[name].wait()
    entries = table.shape[2]
    chunks = [(a, min(a + cols, entries)) for a in range(0, entries, cols)]
    for z in range(depth):
        index = elem[z]
        gate = STEP * mask[z].astype(jnp.float32)
        low, high = index % cols, index // cols
        for i in range(3):
            value = jnp.zeros((rows, cols), jnp.float32)
            for j, (a, b) in enumerate(chunks):
                line = jnp.broadcast_to(table[i, :, pl.ds(a, b - a)], (rows, cols))
                value = jnp.where(high == j, jnp.take_along_axis(line, low, axis=1), value)
            rest[0, i, z] = rest[0, i, z] + gate * value

    def mate_copy(d, part):
        inner, top, bottom = pl.ds(2, rows - 4), pl.ds(0, 2), pl.ds(rows - 2, 2)
        both, last = pl.ds(0, 2), pl.ds(2, 1)
        src, which, lines = (
            (early, last, inner),
            (early, both, inner),
            (mine, last, top),
            (mine, last, bottom),
            (mine, both, top),
            (mine, both, bottom),
            (mine_lanes, None, None),
        )[part]
        if which is None:
            dst = theirs_lanes.at[d]
        else:
            src, dst = src.at[which, :, lines, :], theirs.at[d, which, :, lines, :]
        return pltpu.make_async_remote_copy(
            src_ref=src,
            dst_ref=dst,
            send_sem=ev_send.at[d, part],
            recv_sem=ev_recv.at[d, part],
            device_id=mates[d],
            device_id_type=MESH,
        )

    def to_mates(*parts):
        for d in range(len(mates)):
            for part in parts:
                mate_copy(d, part).start()

    row_diff = (row_behind, row_ahead, row_ahead)
    inner = pl.ds(2, rows - 4)
    force = buoy[:, inner, :] * STEP
    force = jnp.stack([force, -force])
    value = 0.0
    for i in range(3):
        change = force * (sums[i, :, :, inner, :] + row_diff[i](ext, i, rows - 4, 2))
        value = value + (rest[0, i, :, inner, :] + change[0]) * change[1]
    early[2, :, inner, :] = value / STEP
    to_mates(0)

    receive(0, ("up", "down", "left", "right"))
    fix = lane_fix(pack[0], from_left[0], from_right[0], lanes, per, (True, False, True))
    force = buoy[...] * STEP
    force = jnp.stack([force, -force])
    for i in range(3):
        divergence = (
            sums[i]
            + row_diff[i](ext, i, rows)
            + unpack_lanes(fix, i * per, per, depth, edge)
        )
        moved = rest[:, i] + force * divergence
        vext[:, i, :, pl.ds(PAD, rows), :] = moved
        new[0, i] = moved[0]

    velocity = [inside(vext, i) for i in range(3)]
    pack[1] = pack_lanes(velocity, lanes)
    send(1, ("up", "down", "left", "right"))

    def terms(rate_x, rate_y, rate_z, shear_xy, shear_xz, shear_yz):
        dilatation = rate_x + rate_y + rate_z
        modulus = (
            2.0 * (rate_x[0] * rate_x[1] + rate_y[0] * rate_y[1] + rate_z[0] * rate_z[1])
            + shear_xy[0] * shear_xy[1]
            + shear_xz[0] * shear_xz[1]
            + shear_yz[0] * shear_yz[1]
        )
        return dilatation, dilatation[0] * dilatation[1], modulus

    vx, vy, vz = velocity
    mine[2] = (
        vx[0] * (vx[1] - rest[1, 0]) + vy[0] * (vy[1] - rest[1, 1]) + vz[0] * (vz[1] - rest[1, 2])
    ) / STEP
    to_mates(2, 3)

    sums[0] = lane_behind(vx)
    sums[1] = lane_ahead(vy)
    sums[2] = lane_behind(vz) + depth_behind(vy)
    rate_z = depth_ahead(vz)
    shear_xz = depth_behind(vx)

    for i in range(3):
        vint[:, i, :, pl.ds(PAD, rows), :] = velocity[i]
    _, early[0], early[1] = terms(
        row_ahead(vint, 0, rows),
        sums[1],
        rate_z,
        sums[0] + row_behind(vint, 1, rows),
        shear_xz + row_behind(vint, 2, rows),
        sums[2],
    )
    to_mates(1)
    loads["lame"].wait()
    loads["shear"].wait()

    receive(1, ("up", "down", "left", "right"))
    fix = lane_fix(pack[1], from_left[1], from_right[1], lanes, per, (False, True, False))
    rate_x = row_ahead(vext, 0, rows)
    rate_y = sums[1] + unpack_lanes(fix, per, per, depth, edge)
    shear_xy = sums[0] + unpack_lanes(fix, 0, per, depth, edge) + row_behind(vext, 1, rows)
    shear_xz = shear_xz + row_behind(vext, 2, rows)
    shear_yz = sums[2] + unpack_lanes(fix, 2 * per, per, depth, edge)
    dilatation, mine[0], mine[1] = terms(rate_x, rate_y, rate_z, shear_xy, shear_xz, shear_yz)
    to_mates(4, 5)
    mine_lanes[...] = pack_lanes((mine[...],), lanes)
    to_mates(6)

    mu = STEP * shear[...]
    bulk = STEP * lame[...] * dilatation[0]
    new[0, 3] = ext[0, 0, :, pl.ds(PAD, rows), :] + (bulk + 2.0 * mu * rate_x[0])
    new[0, 4] = rest[0, 3] + (bulk + 2.0 * mu * rate_y[0])
    new[0, 5] = rest[0, 4] + (bulk + 2.0 * mu * rate_z[0])
    new[0, 6] = ext[0, 1, :, pl.ds(PAD, rows), :] + mu * shear_xy[0]
    new[0, 7] = ext[0, 2, :, pl.ds(PAD, rows), :] + mu * shear_xz[0]
    new[0, 8] = rest[0, 5] + mu * shear_yz[0]
    for d in range(len(mates)):
        for part in range(7):
            mate_copy(d, part).wait_recv()
    sent(0)
    sent(1)
    for d in range(len(mates)):
        for part in range(7):
            mate_copy(d, part).wait_send()


def finish(n_mates, new_in, mine, theirs, theirs_lanes, out, grad, total, sem):
    state_copy = pltpu.make_async_copy(new_in, out, sem.at[0])
    state_copy.start()
    _, depth, rows, cols = mine.shape
    lanes = lax.broadcasted_iota(jnp.int32, (rows, cols), 1)
    edge = jnp.logical_or(lanes < 2, lanes >= cols - 2)
    for part in range(3):
        for z in range(depth):
            value = mine[part, z]
            for d in range(n_mates):
                last = turn(theirs_lanes[d], -(4 * (part * depth + z) + 2))
                value = value + jnp.where(edge, last, theirs[d, part, z])
            total[part, z] = value
    grad_copy = pltpu.make_async_copy(total, grad, sem.at[1])
    grad_copy.start()
    state_copy.wait()
    grad_copy.wait()


def solution(mesh):
    sizes = (mesh.shape["ev"], mesh.shape["gx"], mesh.shape["gy"])

    def shards(fwd, adj, lame, shear, buoy, mask, elem, table):
        _, _, depth, rows, cols = fwd.shape
        table = jnp.swapaxes(table, 0, 1)
        block = (depth, rows, cols)
        padded = (2, 3, depth, rows + 2 * PAD, cols)
        mates = max(sizes[0] - 1, 1)
        f32 = jnp.float32
        dma = pltpu.SemaphoreType.DMA
        anywhere = pl.BlockSpec(memory_space=pl.ANY)
        whole = pl.BlockSpec(memory_space=pltpu.VMEM)
        new, *pieces = pl.pallas_call(
            functools.partial(kernel, sizes),
            out_shape=(
                pltpu.VMEM(fwd.shape, f32),
                pltpu.VMEM((3,) + block, f32),
                pltpu.VMEM((mates, 3) + block, f32),
                pltpu.VMEM((mates, rows, cols), f32),
            ),
            in_specs=[anywhere] * 8,
            out_specs=(whole,) * 4,
            scratch_shapes=[
                pltpu.VMEM(padded, f32),
                pltpu.VMEM((2, 6) + block, f32),
                pltpu.VMEM(block, f32),
                pltpu.VMEM(block, f32),
                pltpu.VMEM(block, f32),
                pltpu.VMEM(block, jnp.int32),
                pltpu.VMEM(block, jnp.int32),
                pltpu.VMEM(table.shape, f32),
                pltpu.VMEM(padded, f32),
                pltpu.VMEM((3, 2) + block, f32),
                pltpu.VMEM((2, rows, cols), f32),
                pltpu.VMEM((2, rows, cols), f32),
                pltpu.VMEM((2, rows, cols), f32),
                pltpu.VMEM(padded, f32),
                pltpu.VMEM((3,) + block, f32),
                pltpu.VMEM((rows, cols), f32),
                dma((16,)),
                dma((4,)),
                dma((4,)),
                dma((4,)),
                dma((4,)),
                dma((mates, 7)),
                dma((mates, 7)),
            ],
            compiler_params=pltpu.CompilerParams(
                collective_id=0, has_side_effects=True, vmem_limit_bytes=56 * 1024 * 1024
            ),
        )(fwd, adj, lame, shear, buoy, mask, elem, table)
        return pl.pallas_call(
            functools.partial(finish, sizes[0] - 1),
            out_shape=(
                jax.ShapeDtypeStruct(fwd.shape, f32),
                jax.ShapeDtypeStruct((3,) + block, f32),
            ),
            in_specs=[anywhere] + [whole] * 3,
            out_specs=(anywhere, anywhere),
            scratch_shapes=[pltpu.VMEM((3,) + block, f32), dma((2,))],
            compiler_params=pltpu.CompilerParams(vmem_limit_bytes=8 * 1024 * 1024),
        )(new, *pieces)

    grid = P(None, "gx", "gy")
    state = P("ev", None, None, "gx", "gy")
    return jax.shard_map(
        shards,
        mesh=mesh,
        in_specs=(state, state, grid, grid, grid, grid, grid, P("ev", None, None)),
        out_specs=(state, P(None, None, "gx", "gy")),
        check_vma=False,
    )
```

```python
import functools

import jax
import jax.numpy as jnp
from jax import lax
from jax.experimental import pallas as pl
from jax.experimental.pallas import tpu as pltpu
from jax.sharding import PartitionSpec as P

MESH = pl.DeviceIdType.MESH
INNER = 9.0 / 8.0
OUTER = -1.0 / 24.0
STEP = 0.15
PAD = 8


def depth_ahead(f):
    zero = jnp.zeros_like(f[:, :1])
    p1 = jnp.concatenate([f[:, 1:], zero], 1)
    p2 = jnp.concatenate([f[:, 2:], zero, zero], 1)
    m1 = jnp.concatenate([zero, f[:, :-1]], 1)
    return INNER * (p1 - f) + OUTER * (p2 - m1)


def depth_behind(f):
    zero = jnp.zeros_like(f[:, :1])
    p1 = jnp.concatenate([f[:, 1:], zero], 1)
    m1 = jnp.concatenate([zero, f[:, :-1]], 1)
    m2 = jnp.concatenate([zero, zero, f[:, :-2]], 1)
    return INNER * (f - m1) + OUTER * (p1 - m2)


def turn(f, shift):
    return pltpu.roll(f, shift % f.shape[-1], f.ndim - 1)


def lane_ahead(f):
    return INNER * (turn(f, -1) - f) + OUTER * (turn(f, -2) - turn(f, 1))


def lane_behind(f):
    return INNER * (f - turn(f, 1)) + OUTER * (turn(f, -1) - turn(f, 2))


def row_ahead(ref, c, rows, first=0):
    def at(k):
        return ref[:, c, :, pl.ds(PAD + first + k, rows), :]

    return INNER * (at(1) - at(0)) + OUTER * (at(2) - at(-1))


def row_behind(ref, c, rows, first=0):
    def at(k):
        return ref[:, c, :, pl.ds(PAD + first + k, rows), :]

    return INNER * (at(0) - at(-1)) + OUTER * (at(1) - at(-2))


def pack_lanes(fields, lanes):
    slot_of = lanes // 4
    packed = jnp.zeros(lanes.shape, jnp.float32)
    k = 0
    for f in fields:
        for s in range(f.shape[0]):
            for z in range(f.shape[1]):
                packed = jnp.where(slot_of == k, turn(f[s, z], 4 * k + 2), packed)
                k += 1
    return packed


def lane_fix(own, left, right, lanes, per, ahead):
    place = lanes % 4
    kind = lanes // (4 * per)
    is_ahead = functools.reduce(
        jnp.logical_or, [kind == c for c, flag in enumerate(ahead) if flag]
    )

    def weight(ahead_at, behind_at):
        def table(entries):
            out = jnp.zeros(lanes.shape, jnp.float32)
            for j, value in entries:
                out = jnp.where(place == j, value, out)
            return out

        return jnp.where(is_ahead, table(ahead_at), table(behind_at))

    m = jnp.where(place < 2, left, right) - own
    return (
        weight([(0, OUTER), (1, OUTER)], []) * turn(m, -2)
        + weight([(1, INNER)], [(1, OUTER)]) * turn(m, -1)
        + weight([(2, -OUTER)], [(2, -INNER)]) * turn(m, 1)
        + weight([], [(2, -OUTER), (3, -OUTER)]) * turn(m, 2)
    )


def unpack_lanes(fix, first, count, depth, edge):
    parts = []
    for s in range(2):
        parts.append(
            jnp.stack(
                [
                    jnp.where(edge, turn(fix, -(4 * (first + s * depth + z) + 2)), 0.0)
                    for z in range(depth)
                ]
            )
        )
    return jnp.stack(parts)


def kernel(
    sizes,
    fwd,
    adj,
    lame_in,
    shear_in,
    buoy_in,
    mask_in,
    elem_in,
    table_in,
    new,
    mine,
    theirs,
    theirs_rows,
    theirs_lanes,
    ext,
    rest,
    lame,
    shear,
    buoy,
    mask,
    elem,
    table,
    vext,
    sums,
    pack,
    from_left,
    from_right,
    vint,
    early,
    mine_rows,
    mine_lanes,
    row_out,
    row_in,
    load_sem,
    row_send,
    row_recv,
    lane_send,
    lane_recv,
    ev_send,
    ev_recv,
):
    n_ev, n_gx, n_gy = sizes
    ev, gx, gy = lax.axis_index("ev"), lax.axis_index("gx"), lax.axis_index("gy")
    _, _, depth, rows, cols = rest.shape
    per = 2 * depth

    barrier = pltpu.get_barrier_semaphore()
    has = {
        "up": gx > 0,
        "down": gx < n_gx - 1,
        "left": gy > 0,
        "right": gy < n_gy - 1,
    }
    where = {
        "up": {"gx": gx - 1},
        "down": {"gx": gx + 1},
        "left": {"gy": gy - 1},
        "right": {"gy": gy + 1},
    }
    mates = [{"ev": lax.rem(ev + d, n_ev)} for d in range(1, n_ev)]

    for side in has:

        @pl.when(has[side])
        def _(side=side):
            pl.semaphore_signal(barrier, inc=1, device_id=where[side], device_id_type=MESH)

    for mate in mates:
        pl.semaphore_signal(barrier, inc=1, device_id=mate, device_id_type=MESH)

    loads = {}

    def load(name, src, dst):
        copy = pltpu.make_async_copy(src, dst, load_sem.at[len(loads)])
        loads[name] = copy
        copy.start()

    for s, state in enumerate((fwd, adj)):
        load(("n0", s), state.at[0, pl.ds(3, 1)], ext.at[s, pl.ds(0, 1), :, pl.ds(PAD, rows), :])
        load(("n1", s), state.at[0, pl.ds(6, 2)], ext.at[s, pl.ds(1, 2), :, pl.ds(PAD, rows), :])
        load(("s0", s), state.at[0, pl.ds(4, 2)], rest.at[s, pl.ds(3, 2)])
        load(("s1", s), state.at[0, pl.ds(8, 1)], rest.at[s, pl.ds(5, 1)])
    for s, state in enumerate((fwd, adj)):
        load(("v", s), state.at[0, pl.ds(0, 3)], rest.at[s, pl.ds(0, 3)])
    load("table", table_in, table)
    load("elem", elem_in, elem)
    load("mask", mask_in, mask)
    load("buoy", buoy_in, buoy)
    load("lame", lame_in, lame)
    load("shear", shear_in, shear)

    for start in (0, PAD + rows):
        vint[:, :, :, pl.ds(start, PAD), :] = jnp.zeros(vint.shape[:3] + (PAD, cols), jnp.float32)

    @pl.when(gx == 0)
    def _():
        for ref in (ext, vext):
            ref[:, :, :, pl.ds(0, PAD), :] = jnp.zeros(ref.shape[:3] + (PAD, cols), jnp.float32)

    @pl.when(gx == n_gx - 1)
    def _():
        for ref in (ext, vext):
            ref[:, :, :, pl.ds(PAD + rows, PAD), :] = jnp.zeros(
                ref.shape[:3] + (PAD, cols), jnp.float32
            )

    @pl.when(gy == 0)
    def _():
        from_left[...] = jnp.zeros(from_left.shape, jnp.float32)

    @pl.when(gy == n_gy - 1)
    def _():
        from_right[...] = jnp.zeros(from_right.shape, jnp.float32)

    for s in range(2):
        for name in ("n0", "n1", "s0", "s1"):
            loads[name, s].wait()

    lanes = lax.broadcasted_iota(jnp.int32, (rows, cols), 1)
    edge = jnp.logical_or(lanes < 2, lanes >= cols - 2)

    def inside(ref, c):
        return ref[:, c, :, pl.ds(PAD, rows), :]

    def row_copy(phase, side):
        i = int(side == "down")
        return pltpu.make_async_remote_copy(
            src_ref=row_out.at[phase, i],
            dst_ref=row_in.at[phase, i],
            send_sem=row_send.at[2 * phase + i],
            recv_sem=row_recv.at[2 * phase + i],
            device_id=where[side],
            device_id_type=MESH,
        )

    def lane_copy(phase, side):
        i = 2 * phase + (side == "right")
        return pltpu.make_async_remote_copy(
            src_ref=pack.at[phase],
            dst_ref=(from_left if side == "right" else from_right).at[phase],
            send_sem=lane_send.at[i],
            recv_sem=lane_recv.at[i],
            device_id=where[side],
            device_id_type=MESH,
        )

    opposite = {"up": "down", "down": "up", "left": "right", "right": "left"}

    def copy_of(phase, side):
        if side in ("up", "down"):
            return row_copy(phase, side)
        return lane_copy(phase, side)

    def send(phase, sides):
        for i, start in enumerate((PAD, PAD + rows - 2)):
            row_out[phase, i] = (ext, vext)[phase][:, :, :, pl.ds(start, 2), :]
        for side in sides:

            @pl.when(has[side])
            def _(side=side):
                copy_of(phase, side).start()

    def receive(phase, sides):
        for side in sides:

            @pl.when(has[side])
            def _(side=side):
                copy_of(phase, opposite[side]).wait_recv()
                if side in ("up", "down"):
                    i, goal = (1, PAD - 2) if side == "up" else (0, PAD + rows)
                    (ext, vext)[phase][:, :, :, pl.ds(goal, 2), :] = row_in[phase, i]

    def sent(phase):
        for side in has:

            @pl.when(has[side])
            def _(side=side):
                copy_of(phase, side).wait_send()

    sxy, syy, syz = inside(ext, 1), rest[:, 3], rest[:, 5]
    pack[0] = pack_lanes((sxy, syy, syz), lanes)

    peers = len(mates) + sum(flag.astype(jnp.int32) for flag in has.values())
    pl.semaphore_wait(barrier, peers)

    send(0, ("up", "down", "left", "right"))

    sums[0] = lane_ahead(sxy) + depth_ahead(inside(ext, 2))
    sums[1] = lane_behind(syy) + depth_ahead(syz)
    sums[2] = lane_ahead(syz) + depth_behind(rest[:, 4])

    for name in (("v", 0), ("v", 1), "table", "elem", "mask", "buoy"):
        loads[name].wait()
    entries = table.shape[2]
    chunks = [(a, min(a + cols, entries)) for a in range(0, entries, cols)]
    for z in range(depth):
        index = elem[z]
        gate = STEP * mask[z].astype(jnp.float32)
        low, high = index % cols, index // cols
        for i in range(3):
            value = jnp.zeros((rows, cols), jnp.float32)
            for j, (a, b) in enumerate(chunks):
                line = jnp.broadcast_to(table[i, :, pl.ds(a, b - a)], (rows, cols))
                value = jnp.where(high == j, jnp.take_along_axis(line, low, axis=1), value)
            rest[0, i, z] = rest[0, i, z] + gate * value

    def mate_copy(d, part):
        src, dst = (
            (early.at[2], theirs.at[d, 2]),
            (early.at[pl.ds(0, 2)], theirs.at[d, pl.ds(0, 2)]),
            (mine_rows, theirs_rows.at[d]),
            (mine_lanes, theirs_lanes.at[d]),
        )[part]
        return pltpu.make_async_remote_copy(
            src_ref=src,
            dst_ref=dst,
            send_sem=ev_send.at[d, part],
            recv_sem=ev_recv.at[d, part],
            device_id=mates[d],
            device_id_type=MESH,
        )

    def to_mates(*parts):
        for d in range(len(mates)):
            for part in parts:
                mate_copy(d, part).start()

    row_diff = (row_behind, row_ahead, row_ahead)
    inner = pl.ds(2, rows - 4)
    force = buoy[:, inner, :] * STEP
    force = jnp.stack([force, -force])
    value = 0.0
    for i in range(3):
        change = force * (sums[i, :, :, inner, :] + row_diff[i](ext, i, rows - 4, 2))
        value = value + (rest[0, i, :, inner, :] + change[0]) * change[1]
    early[2, :, pl.ds(0, 2), :] = jnp.zeros((depth, 2, cols), jnp.float32)
    early[2, :, pl.ds(rows - 2, 2), :] = jnp.zeros((depth, 2, cols), jnp.float32)
    early[2, :, inner, :] = value / STEP
    to_mates(0)

    receive(0, ("up", "down", "left", "right"))
    fix = lane_fix(pack[0], from_left[0], from_right[0], lanes, per, (True, False, True))
    force = buoy[...] * STEP
    force = jnp.stack([force, -force])
    for i in range(3):
        divergence = (
            sums[i]
            + row_diff[i](ext, i, rows)
            + unpack_lanes(fix, i * per, per, depth, edge)
        )
        moved = rest[:, i] + force * divergence
        vext[:, i, :, pl.ds(PAD, rows), :] = moved
        new[0, i] = moved[0]

    velocity = [inside(vext, i) for i in range(3)]
    pack[1] = pack_lanes(velocity, lanes)
    send(1, ("up", "down", "left", "right"))

    def terms(rate_x, rate_y, rate_z, shear_xy, shear_xz, shear_yz):
        dilatation = rate_x + rate_y + rate_z
        modulus = (
            2.0 * (rate_x[0] * rate_x[1] + rate_y[0] * rate_y[1] + rate_z[0] * rate_z[1])
            + shear_xy[0] * shear_xy[1]
            + shear_xz[0] * shear_xz[1]
            + shear_yz[0] * shear_yz[1]
        )
        return dilatation, dilatation[0] * dilatation[1], modulus

    vx, vy, vz = velocity
    mine[2] = (
        vx[0] * (vx[1] - rest[1, 0]) + vy[0] * (vy[1] - rest[1, 1]) + vz[0] * (vz[1] - rest[1, 2])
    ) / STEP
    sums[0] = lane_behind(vx)
    sums[1] = lane_ahead(vy)
    sums[2] = lane_behind(vz) + depth_behind(vy)
    rate_z = depth_ahead(vz)
    shear_xz = depth_behind(vx)

    for i in range(3):
        vint[:, i, :, pl.ds(PAD, rows), :] = velocity[i]
    _, early[0], early[1] = terms(
        row_ahead(vint, 0, rows),
        sums[1],
        rate_z,
        sums[0] + row_behind(vint, 1, rows),
        shear_xz + row_behind(vint, 2, rows),
        sums[2],
    )
    to_mates(1)
    loads["lame"].wait()
    loads["shear"].wait()

    receive(1, ("up", "down", "left", "right"))
    fix = lane_fix(pack[1], from_left[1], from_right[1], lanes, per, (False, True, False))
    rate_x = row_ahead(vext, 0, rows)
    rate_y = sums[1] + unpack_lanes(fix, per, per, depth, edge)
    shear_xy = sums[0] + unpack_lanes(fix, 0, per, depth, edge) + row_behind(vext, 1, rows)
    shear_xz = shear_xz + row_behind(vext, 2, rows)
    shear_yz = sums[2] + unpack_lanes(fix, 2 * per, per, depth, edge)
    dilatation, mine[0], mine[1] = terms(rate_x, rate_y, rate_z, shear_xy, shear_xz, shear_yz)
    for i, start in enumerate((0, rows - 2)):
        mine_rows[:, :, pl.ds(2 * i, 2), :] = mine[:, :, pl.ds(start, 2), :]
    to_mates(2)
    mine_lanes[...] = pack_lanes((mine[...],), lanes)
    to_mates(3)

    mu = STEP * shear[...]
    bulk = STEP * lame[...] * dilatation[0]
    new[0, 3] = ext[0, 0, :, pl.ds(PAD, rows), :] + (bulk + 2.0 * mu * rate_x[0])
    new[0, 4] = rest[0, 3] + (bulk + 2.0 * mu * rate_y[0])
    new[0, 5] = rest[0, 4] + (bulk + 2.0 * mu * rate_z[0])
    new[0, 6] = ext[0, 1, :, pl.ds(PAD, rows), :] + mu * shear_xy[0]
    new[0, 7] = ext[0, 2, :, pl.ds(PAD, rows), :] + mu * shear_xz[0]
    new[0, 8] = rest[0, 5] + mu * shear_yz[0]
    for d in range(len(mates)):
        for part in range(4):
            mate_copy(d, part).wait_recv()
    sent(0)
    sent(1)
    for d in range(len(mates)):
        for part in range(4):
            mate_copy(d, part).wait_send()


def finish(n_mates, new_in, mine, theirs, theirs_rows, theirs_lanes, out, grad, total, sem):
    state_copy = pltpu.make_async_copy(new_in, out, sem.at[0])
    state_copy.start()
    _, depth, rows, cols = mine.shape
    lanes = lax.broadcasted_iota(jnp.int32, (rows, cols), 1)
    edge = jnp.logical_or(lanes < 2, lanes >= cols - 2)
    for part in range(3):
        for z in range(depth):
            value = mine[part, z]
            for d in range(n_mates):
                last = turn(theirs_lanes[d], -(4 * (part * depth + z) + 2))
                value = value + jnp.where(edge, last, theirs[d, part, z])
            total[part, z] = value
    if n_mates:
        for i, start in enumerate((0, rows - 2)):
            value = mine[:, :, pl.ds(start, 2), :]
            for d in range(n_mates):
                value = value + theirs_rows[d, :, :, pl.ds(2 * i, 2), :]
            total[:, :, pl.ds(start, 2), :] = value
    grad_copy = pltpu.make_async_copy(total, grad, sem.at[1])
    grad_copy.start()
    state_copy.wait()
    grad_copy.wait()


def solution(mesh):
    sizes = (mesh.shape["ev"], mesh.shape["gx"], mesh.shape["gy"])

    def shards(fwd, adj, lame, shear, buoy, mask, elem, table):
        _, _, depth, rows, cols = fwd.shape
        table = jnp.swapaxes(table, 0, 1)
        block = (depth, rows, cols)
        padded = (2, 3, depth, rows + 2 * PAD, cols)
        mates = max(sizes[0] - 1, 1)
        f32 = jnp.float32
        dma = pltpu.SemaphoreType.DMA
        anywhere = pl.BlockSpec(memory_space=pl.ANY)
        whole = pl.BlockSpec(memory_space=pltpu.VMEM)
        new, *pieces = pl.pallas_call(
            functools.partial(kernel, sizes),
            out_shape=(
                pltpu.VMEM(fwd.shape, f32),
                pltpu.VMEM((3,) + block, f32),
                pltpu.VMEM((mates, 3) + block, f32),
                pltpu.VMEM((mates, 3, depth, 4, cols), f32),
                pltpu.VMEM((mates, rows, cols), f32),
            ),
            in_specs=[anywhere] * 8,
            out_specs=(whole,) * 5,
            scratch_shapes=[
                pltpu.VMEM(padded, f32),
                pltpu.VMEM((2, 6) + block, f32),
                pltpu.VMEM(block, f32),
                pltpu.VMEM(block, f32),
                pltpu.VMEM(block, f32),
                pltpu.VMEM(block, jnp.int32),
                pltpu.VMEM(block, jnp.int32),
                pltpu.VMEM(table.shape, f32),
                pltpu.VMEM(padded, f32),
                pltpu.VMEM((3, 2) + block, f32),
                pltpu.VMEM((2, rows, cols), f32),
                pltpu.VMEM((2, rows, cols), f32),
                pltpu.VMEM((2, rows, cols), f32),
                pltpu.VMEM(padded, f32),
                pltpu.VMEM((3,) + block, f32),
                pltpu.VMEM((3, depth, 4, cols), f32),
                pltpu.VMEM((rows, cols), f32),
                pltpu.VMEM((2, 2, 2, 3, depth, 2, cols), f32),
                pltpu.VMEM((2, 2, 2, 3, depth, 2, cols), f32),
                dma((16,)),
                dma((4,)),
                dma((4,)),
                dma((4,)),
                dma((4,)),
                dma((mates, 4)),
                dma((mates, 4)),
            ],
            compiler_params=pltpu.CompilerParams(
                collective_id=0, has_side_effects=True, vmem_limit_bytes=56 * 1024 * 1024
            ),
        )(fwd, adj, lame, shear, buoy, mask, elem, table)
        return pl.pallas_call(
            functools.partial(finish, sizes[0] - 1),
            out_shape=(
                jax.ShapeDtypeStruct(fwd.shape, f32),
                jax.ShapeDtypeStruct((3,) + block, f32),
            ),
            in_specs=[anywhere] + [whole] * 4,
            out_specs=(anywhere, anywhere),
            scratch_shapes=[pltpu.VMEM((3,) + block, f32), dma((2,))],
            compiler_params=pltpu.CompilerParams(vmem_limit_bytes=8 * 1024 * 1024),
        )(new, *pieces)

    grid = P(None, "gx", "gy")
    state = P("ev", None, None, "gx", "gy")
    return jax.shard_map(
        shards,
        mesh=mesh,
        in_specs=(state, state, grid, grid, grid, grid, grid, P("ev", None, None)),
        out_specs=(state, P(None, None, "gx", "gy")),
        check_vma=False,
    )
```

```python
import functools

import jax
import jax.numpy as jnp
from jax import lax
from jax.experimental import pallas as pl
from jax.experimental.pallas import tpu as pltpu
from jax.sharding import PartitionSpec as P

MESH = pl.DeviceIdType.MESH
INNER = 9.0 / 8.0
OUTER = -1.0 / 24.0
STEP = 0.15
PAD = 8


def depth_ahead(f):
    zero = jnp.zeros_like(f[:, :1])
    p1 = jnp.concatenate([f[:, 1:], zero], 1)
    p2 = jnp.concatenate([f[:, 2:], zero, zero], 1)
    m1 = jnp.concatenate([zero, f[:, :-1]], 1)
    return INNER * (p1 - f) + OUTER * (p2 - m1)


def depth_behind(f):
    zero = jnp.zeros_like(f[:, :1])
    p1 = jnp.concatenate([f[:, 1:], zero], 1)
    m1 = jnp.concatenate([zero, f[:, :-1]], 1)
    m2 = jnp.concatenate([zero, zero, f[:, :-2]], 1)
    return INNER * (f - m1) + OUTER * (p1 - m2)


def turn(f, shift):
    return pltpu.roll(f, shift % f.shape[-1], f.ndim - 1)


def lane_ahead(f):
    return INNER * (turn(f, -1) - f) + OUTER * (turn(f, -2) - turn(f, 1))


def lane_behind(f):
    return INNER * (f - turn(f, 1)) + OUTER * (turn(f, -1) - turn(f, 2))


def row_ahead(ref, c, rows):
    def at(k):
        return ref[:, c, :, pl.ds(PAD + k, rows), :]

    return INNER * (at(1) - at(0)) + OUTER * (at(2) - at(-1))


def row_behind(ref, c, rows):
    def at(k):
        return ref[:, c, :, pl.ds(PAD + k, rows), :]

    return INNER * (at(0) - at(-1)) + OUTER * (at(1) - at(-2))


def pack_lanes(fields, lanes):
    slot_of = lanes // 4
    packed = jnp.zeros(lanes.shape, jnp.float32)
    k = 0
    for f in fields:
        for s in range(f.shape[0]):
            for z in range(f.shape[1]):
                packed = jnp.where(slot_of == k, turn(f[s, z], 4 * k + 2), packed)
                k += 1
    return packed


def lane_fix(own, left, right, lanes, per, ahead):
    place = lanes % 4
    kind = lanes // (4 * per)
    is_ahead = functools.reduce(
        jnp.logical_or, [kind == c for c, flag in enumerate(ahead) if flag]
    )

    def weight(ahead_at, behind_at):
        def table(entries):
            out = jnp.zeros(lanes.shape, jnp.float32)
            for j, value in entries:
                out = jnp.where(place == j, value, out)
            return out

        return jnp.where(is_ahead, table(ahead_at), table(behind_at))

    m = jnp.where(place < 2, left, right) - own
    return (
        weight([(0, OUTER), (1, OUTER)], []) * turn(m, -2)
        + weight([(1, INNER)], [(1, OUTER)]) * turn(m, -1)
        + weight([(2, -OUTER)], [(2, -INNER)]) * turn(m, 1)
        + weight([], [(2, -OUTER), (3, -OUTER)]) * turn(m, 2)
    )


def unpack_lanes(fix, first, count, depth, edge):
    parts = []
    for s in range(2):
        parts.append(
            jnp.stack(
                [
                    jnp.where(edge, turn(fix, -(4 * (first + s * depth + z) + 2)), 0.0)
                    for z in range(depth)
                ]
            )
        )
    return jnp.stack(parts)


def kernel(
    sizes,
    fwd,
    adj,
    lame_in,
    shear_in,
    buoy_in,
    mask_in,
    elem_in,
    table_in,
    new,
    mine,
    theirs,
    theirs_rows,
    theirs_lanes,
    ext,
    rest,
    lame,
    shear,
    buoy,
    mask,
    elem,
    table,
    vext,
    sums,
    pack,
    from_left,
    from_right,
    vint,
    early,
    mine_lanes,
    load_sem,
    row_send,
    row_recv,
    lane_send,
    lane_recv,
    ev_send,
    ev_recv,
):
    n_ev, n_gx, n_gy = sizes
    ev, gx, gy = lax.axis_index("ev"), lax.axis_index("gx"), lax.axis_index("gy")
    _, _, depth, rows, cols = rest.shape
    per = 2 * depth

    barrier = pltpu.get_barrier_semaphore()
    has = {
        "up": gx > 0,
        "down": gx < n_gx - 1,
        "left": gy > 0,
        "right": gy < n_gy - 1,
    }
    where = {
        "up": {"gx": gx - 1},
        "down": {"gx": gx + 1},
        "left": {"gy": gy - 1},
        "right": {"gy": gy + 1},
    }
    mates = [{"ev": lax.rem(ev + d, n_ev)} for d in range(1, n_ev)]

    for side in has:

        @pl.when(has[side])
        def _(side=side):
            pl.semaphore_signal(barrier, inc=1, device_id=where[side], device_id_type=MESH)

    for mate in mates:
        pl.semaphore_signal(barrier, inc=1, device_id=mate, device_id_type=MESH)

    loads = {}

    def load(name, src, dst):
        copy = pltpu.make_async_copy(src, dst, load_sem.at[len(loads)])
        loads[name] = copy
        copy.start()

    for s, state in enumerate((fwd, adj)):
        load(("n0", s), state.at[0, pl.ds(3, 1)], ext.at[s, pl.ds(0, 1), :, pl.ds(PAD, rows), :])
        load(("n1", s), state.at[0, pl.ds(6, 2)], ext.at[s, pl.ds(1, 2), :, pl.ds(PAD, rows), :])
        load(("s0", s), state.at[0, pl.ds(4, 2)], rest.at[s, pl.ds(3, 2)])
        load(("s1", s), state.at[0, pl.ds(8, 1)], rest.at[s, pl.ds(5, 1)])
    @pl.when(gx == 0)
    def _():
        for ref in (ext, vext):
            ref[:, :, :, pl.ds(0, PAD), :] = jnp.zeros(ref.shape[:3] + (PAD, cols), jnp.float32)

    @pl.when(gx == n_gx - 1)
    def _():
        for ref in (ext, vext):
            ref[:, :, :, pl.ds(PAD + rows, PAD), :] = jnp.zeros(
                ref.shape[:3] + (PAD, cols), jnp.float32
            )

    @pl.when(gy == 0)
    def _():
        from_left[...] = jnp.zeros(from_left.shape, jnp.float32)

    @pl.when(gy == n_gy - 1)
    def _():
        from_right[...] = jnp.zeros(from_right.shape, jnp.float32)

    for s in range(2):
        for name in ("n0", "n1", "s0", "s1"):
            loads[name, s].wait()

    lanes = lax.broadcasted_iota(jnp.int32, (rows, cols), 1)
    edge = jnp.logical_or(lanes < 2, lanes >= cols - 2)

    def inside(ref, c):
        return ref[:, c, :, pl.ds(PAD, rows), :]

    def row_copy(ref, phase, side):
        start, goal = (PAD + rows - 2, PAD - 2) if side == "down" else (PAD, PAD + rows)
        i = 2 * phase + (side == "down")
        return pltpu.make_async_remote_copy(
            src_ref=ref.at[:, :, :, pl.ds(start, 2), :],
            dst_ref=ref.at[:, :, :, pl.ds(goal, 2), :],
            send_sem=row_send.at[i],
            recv_sem=row_recv.at[i],
            device_id=where[side],
            device_id_type=MESH,
        )

    def lane_copy(phase, side):
        i = 2 * phase + (side == "right")
        return pltpu.make_async_remote_copy(
            src_ref=pack.at[phase],
            dst_ref=(from_left if side == "right" else from_right).at[phase],
            send_sem=lane_send.at[i],
            recv_sem=lane_recv.at[i],
            device_id=where[side],
            device_id_type=MESH,
        )

    opposite = {"up": "down", "down": "up", "left": "right", "right": "left"}

    def copy_of(phase, side):
        if side in ("up", "down"):
            return row_copy((ext, vext)[phase], phase, side)
        return lane_copy(phase, side)

    def send(phase, sides):
        for side in sides:

            @pl.when(has[side])
            def _(side=side):
                copy_of(phase, side).start()

    def receive(phase, sides):
        for side in sides:

            @pl.when(has[side])
            def _(side=side):
                copy_of(phase, opposite[side]).wait_recv()

    def sent(phase):
        for side in has:

            @pl.when(has[side])
            def _(side=side):
                copy_of(phase, side).wait_send()

    sxy, syy, syz = inside(ext, 1), rest[:, 3], rest[:, 5]
    pack[0] = pack_lanes((sxy, syy, syz), lanes)

    peers = len(mates) + sum(flag.astype(jnp.int32) for flag in has.values())
    pl.semaphore_wait(barrier, peers)

    send(0, ("up", "down", "left", "right"))

    for s, state in enumerate((fwd, adj)):
        load(("v", s), state.at[0, pl.ds(0, 3)], rest.at[s, pl.ds(0, 3)])
    load("table", table_in, table)
    load("elem", elem_in, elem)
    load("mask", mask_in, mask)
    load("buoy", buoy_in, buoy)
    load("lame", lame_in, lame)
    load("shear", shear_in, shear)

    for start in (0, PAD + rows):
        vint[:, :, :, pl.ds(start, PAD), :] = jnp.zeros(vint.shape[:3] + (PAD, cols), jnp.float32)

    sums[0] = lane_ahead(sxy) + depth_ahead(inside(ext, 2))
    sums[1] = lane_behind(syy) + depth_ahead(syz)
    sums[2] = lane_ahead(syz) + depth_behind(rest[:, 4])

    for name in (("v", 0), ("v", 1), "table", "elem", "mask", "buoy"):
        loads[name].wait()
    entries = table.shape[2]
    chunks = [(a, min(a + cols, entries)) for a in range(0, entries, cols)]
    for z in range(depth):
        index = elem[z]
        gate = STEP * mask[z].astype(jnp.float32)
        low, high = index % cols, index // cols
        for i in range(3):
            value = jnp.zeros((rows, cols), jnp.float32)
            for j, (a, b) in enumerate(chunks):
                line = jnp.broadcast_to(table[i, :, pl.ds(a, b - a)], (rows, cols))
                value = jnp.where(high == j, jnp.take_along_axis(line, low, axis=1), value)
            rest[0, i, z] = rest[0, i, z] + gate * value

    receive(0, ("up", "down", "left", "right"))
    fix = lane_fix(pack[0], from_left[0], from_right[0], lanes, per, (True, False, True))
    force = buoy[...] * STEP
    force = jnp.stack([force, -force])
    row_diff = (row_behind, row_ahead, row_ahead)
    for i in range(3):
        divergence = (
            sums[i]
            + row_diff[i](ext, i, rows)
            + unpack_lanes(fix, i * per, per, depth, edge)
        )
        moved = rest[:, i] + force * divergence
        vext[:, i, :, pl.ds(PAD, rows), :] = moved
        new[0, i] = moved[0]

    velocity = [inside(vext, i) for i in range(3)]
    pack[1] = pack_lanes(velocity, lanes)
    send(1, ("up", "down", "left", "right"))

    def mate_copy(d, part):
        top, bottom = pl.ds(0, 2), pl.ds(rows - 2, 2)
        both = pl.ds(0, 2)
        src, dst = (
            (mine.at[2], theirs.at[d, 2]),
            (early, theirs.at[d, both]),
            (mine.at[both, :, top, :], theirs_rows.at[d, :, :, top, :]),
            (mine.at[both, :, bottom, :], theirs_rows.at[d, :, :, bottom, :]),
            (mine_lanes, theirs_lanes.at[d]),
        )[part]
        return pltpu.make_async_remote_copy(
            src_ref=src,
            dst_ref=dst,
            send_sem=ev_send.at[d, part],
            recv_sem=ev_recv.at[d, part],
            device_id=mates[d],
            device_id_type=MESH,
        )

    def to_mates(*parts):
        for d in range(len(mates)):
            for part in parts:
                mate_copy(d, part).start()

    def terms(rate_x, rate_y, rate_z, shear_xy, shear_xz, shear_yz):
        dilatation = rate_x + rate_y + rate_z
        modulus = (
            2.0 * (rate_x[0] * rate_x[1] + rate_y[0] * rate_y[1] + rate_z[0] * rate_z[1])
            + shear_xy[0] * shear_xy[1]
            + shear_xz[0] * shear_xz[1]
            + shear_yz[0] * shear_yz[1]
        )
        return dilatation, dilatation[0] * dilatation[1], modulus

    vx, vy, vz = velocity
    mine[2] = (
        vx[0] * (vx[1] - rest[1, 0]) + vy[0] * (vy[1] - rest[1, 1]) + vz[0] * (vz[1] - rest[1, 2])
    ) / STEP
    to_mates(0)

    sums[0] = lane_behind(vx)
    sums[1] = lane_ahead(vy)
    sums[2] = lane_behind(vz) + depth_behind(vy)
    rate_z = depth_ahead(vz)
    shear_xz = depth_behind(vx)

    for i in range(3):
        vint[:, i, :, pl.ds(PAD, rows), :] = velocity[i]
    _, early[0], early[1] = terms(
        row_ahead(vint, 0, rows),
        sums[1],
        rate_z,
        sums[0] + row_behind(vint, 1, rows),
        shear_xz + row_behind(vint, 2, rows),
        sums[2],
    )
    to_mates(1)
    loads["lame"].wait()
    loads["shear"].wait()

    receive(1, ("up", "down", "left", "right"))
    fix = lane_fix(pack[1], from_left[1], from_right[1], lanes, per, (False, True, False))
    rate_x = row_ahead(vext, 0, rows)
    rate_y = sums[1] + unpack_lanes(fix, per, per, depth, edge)
    shear_xy = sums[0] + unpack_lanes(fix, 0, per, depth, edge) + row_behind(vext, 1, rows)
    shear_xz = shear_xz + row_behind(vext, 2, rows)
    shear_yz = sums[2] + unpack_lanes(fix, 2 * per, per, depth, edge)
    dilatation, mine[0], mine[1] = terms(rate_x, rate_y, rate_z, shear_xy, shear_xz, shear_yz)
    to_mates(2, 3)
    mine_lanes[...] = pack_lanes((mine[pl.ds(0, 2)],), lanes)
    to_mates(4)

    mu = STEP * shear[...]
    bulk = STEP * lame[...] * dilatation[0]
    new[0, 3] = ext[0, 0, :, pl.ds(PAD, rows), :] + (bulk + 2.0 * mu * rate_x[0])
    new[0, 4] = rest[0, 3] + (bulk + 2.0 * mu * rate_y[0])
    new[0, 5] = rest[0, 4] + (bulk + 2.0 * mu * rate_z[0])
    new[0, 6] = ext[0, 1, :, pl.ds(PAD, rows), :] + mu * shear_xy[0]
    new[0, 7] = ext[0, 2, :, pl.ds(PAD, rows), :] + mu * shear_xz[0]
    new[0, 8] = rest[0, 5] + mu * shear_yz[0]
    for d in range(len(mates)):
        for part in range(5):
            mate_copy(d, part).wait_recv()
    sent(0)
    sent(1)
    for d in range(len(mates)):
        for part in range(5):
            mate_copy(d, part).wait_send()


def finish(n_mates, new_in, mine, theirs, theirs_rows, theirs_lanes, out, grad, total, sem):
    state_copy = pltpu.make_async_copy(new_in, out, sem.at[0])
    state_copy.start()
    _, depth, rows, cols = mine.shape
    lanes = lax.broadcasted_iota(jnp.int32, (rows, cols), 1)
    edge = jnp.logical_or(lanes < 2, lanes >= cols - 2)
    for part in range(3):
        for z in range(depth):
            value = mine[part, z]
            for d in range(n_mates):
                other = theirs[d, part, z]
                if part < 2:
                    last = turn(theirs_lanes[d], -(4 * (part * depth + z) + 2))
                    other = jnp.where(edge, last, other)
                value = value + other
            total[part, z] = value
    if n_mates:
        for start in (0, rows - 2):
            ends = pl.ds(start, 2)
            value = mine[pl.ds(0, 2), :, ends, :]
            for d in range(n_mates):
                value = value + theirs_rows[d, :, :, ends, :]
            total[pl.ds(0, 2), :, ends, :] = value
    grad_copy = pltpu.make_async_copy(total, grad, sem.at[1])
    grad_copy.start()
    state_copy.wait()
    grad_copy.wait()


def solution(mesh):
    sizes = (mesh.shape["ev"], mesh.shape["gx"], mesh.shape["gy"])

    def shards(fwd, adj, lame, shear, buoy, mask, elem, table):
        _, _, depth, rows, cols = fwd.shape
        table = jnp.swapaxes(table, 0, 1)
        block = (depth, rows, cols)
        padded = (2, 3, depth, rows + 2 * PAD, cols)
        mates = max(sizes[0] - 1, 1)
        f32 = jnp.float32
        dma = pltpu.SemaphoreType.DMA
        anywhere = pl.BlockSpec(memory_space=pl.ANY)
        whole = pl.BlockSpec(memory_space=pltpu.VMEM)
        new, *pieces = pl.pallas_call(
            functools.partial(kernel, sizes),
            out_shape=(
                pltpu.VMEM(fwd.shape, f32),
                pltpu.VMEM((3,) + block, f32),
                pltpu.VMEM((mates, 3) + block, f32),
                pltpu.VMEM((mates, 2) + block, f32),
                pltpu.VMEM((mates, rows, cols), f32),
            ),
            in_specs=[anywhere] * 8,
            out_specs=(whole,) * 5,
            scratch_shapes=[
                pltpu.VMEM(padded, f32),
                pltpu.VMEM((2, 6) + block, f32),
                pltpu.VMEM(block, f32),
                pltpu.VMEM(block, f32),
                pltpu.VMEM(block, f32),
                pltpu.VMEM(block, jnp.int32),
                pltpu.VMEM(block, jnp.int32),
                pltpu.VMEM(table.shape, f32),
                pltpu.VMEM(padded, f32),
                pltpu.VMEM((3, 2) + block, f32),
                pltpu.VMEM((2, rows, cols), f32),
                pltpu.VMEM((2, rows, cols), f32),
                pltpu.VMEM((2, rows, cols), f32),
                pltpu.VMEM(padded, f32),
                pltpu.VMEM((2,) + block, f32),
                pltpu.VMEM((rows, cols), f32),
                dma((16,)),
                dma((4,)),
                dma((4,)),
                dma((4,)),
                dma((4,)),
                dma((mates, 5)),
                dma((mates, 5)),
            ],
            compiler_params=pltpu.CompilerParams(
                collective_id=0, has_side_effects=True, vmem_limit_bytes=56 * 1024 * 1024
            ),
        )(fwd, adj, lame, shear, buoy, mask, elem, table)
        return pl.pallas_call(
            functools.partial(finish, sizes[0] - 1),
            out_shape=(
                jax.ShapeDtypeStruct(fwd.shape, f32),
                jax.ShapeDtypeStruct((3,) + block, f32),
            ),
            in_specs=[anywhere] + [whole] * 4,
            out_specs=(anywhere, anywhere),
            scratch_shapes=[pltpu.VMEM((3,) + block, f32), dma((2,))],
            compiler_params=pltpu.CompilerParams(vmem_limit_bytes=8 * 1024 * 1024),
        )(new, *pieces)

    grid = P(None, "gx", "gy")
    state = P("ev", None, None, "gx", "gy")
    return jax.shard_map(
        shards,
        mesh=mesh,
        in_specs=(state, state, grid, grid, grid, grid, grid, P("ev", None, None)),
        out_specs=(state, P(None, None, "gx", "gy")),
        check_vma=False,
    )
```
